128 devices in a mesh: gz: 4 (over z_lo, core), gy: 8 (over z_hi, x), vec: 4 (over y).
Axes of the slice: x: 4, y: 4, z: 4 (z_hi: 2, z_lo: 2; z = z_hi * 2 + z_lo), core: 2. Of those that a mesh axis runs over, the one named last changes fastest.
Arguments:
- vectors: bfloat16 [256, 3, 32, 16, 128], P('vec', None, 'gz', 'gy'), may hold values from -6 to 6
- links: bfloat16 [3, 3, 3, 32, 16, 128], P(None, None, None, 'gz', 'gy'), may hold values from -4 to 4
- momentum: int32 [3], replicated, may hold values from -5 to 5, as said below
- directions: int32 [3], replicated, may hold values from 0 to 2, each once
Outputs:
- elementals: float32 [4, 2, 256, 256], P(None, None, 'vec')
The draws below stay inside these ranges and needn't reach their ends.
Inputs may be any that keep to these rules, and one draw needn't show every extreme that they name: `momentum`: one component is -5, another 5. `directions`: each of 0, 1, 2 once.
All inputs are finite; a program needn't handle non-finite values.
Results may differ from the reference program's by a relative error of at most 0.0029.
Values may be sent and summed in bfloat16 or wider, within the bound.
No kernel may reach another device: no remote copies, remote signals or barrier semaphores. Data moves between devices by JAX's collectives and lax.ppermute only.
A program may use at most 128 MiB of HBM per device.

```python
import math
import jax
import jax.numpy as jnp
from jax import lax

NEV = 256
LX = 64
NY = 16
NZ = 32


def draw_momentum(key, part):
    first_key = jax.random.fold_in(key, 11)
    second_key = jax.random.fold_in(key, 23)
    middle = jax.random.randint(first_key, (1,), -5, 6, dtype=jnp.int32)
    values = jnp.concatenate([jnp.array([-5, 5], dtype=jnp.int32), middle])
    order = jax.random.permutation(second_key, 3)
    return values[order].astype(jnp.int32)


def block_scale(stream_key, extent, cuts, smallest, largest):
    loudness, own = 1.0, jax.random.fold_in(stream_key, 6)
    for position, blocks in cuts:
        heights = jnp.exp(jax.random.uniform(jax.random.fold_in(own, position), (blocks,), jnp.float32, smallest / len(cuts), largest / len(cuts)))
        loudness = loudness * jnp.repeat(heights, extent[position] // blocks).reshape([-1 if axis == position else 1 for axis in range(len(extent))])
    return loudness


def gaussian(stream_key, dims, deviation, bound, pieces=(), kind=jnp.bfloat16):
    factor_of = block_scale(stream_key, dims, pieces, -0.22, 0.18) if pieces else 1.0
    drawn = jax.random.normal(stream_key, dims, jnp.float32) * deviation * factor_of
    return jnp.minimum(jnp.maximum(drawn, -bound), bound).astype(kind)


def setup_inputs(seed: int = 0) -> dict:
    arg_keys = jax.random.split(jax.random.key(seed), 5)
    return {
        "vectors": gaussian(arg_keys[0], (NEV, 3, NZ, NY, 2 * LX), 1.0, 6.0, ((0, 4), (2, 4), (3, 8))),
        "links": gaussian(arg_keys[1], (3, 3, 3, NZ, NY, 2 * LX), 0.58, 4.0, ((3, 4), (4, 8))),
        "momentum": draw_momentum(jax.random.fold_in(arg_keys[4], 71), 0),
        "directions": jax.random.permutation(arg_keys[3], 3).astype(jnp.int32),
    }


def apply_link(link_pair, field_pair):
    link_real, link_imag = link_pair
    field_real, field_imag = field_pair
    out_real = 0.0
    out_imag = 0.0
    for column in range(3):
        coeff_real = link_real[:, column][None]
        coeff_imag = link_imag[:, column][None]
        value_real = field_real[:, column][:, None]
        value_imag = field_imag[:, column][:, None]
        out_real = out_real + coeff_real * value_real - coeff_imag * value_imag
        out_imag = out_imag + coeff_real * value_imag + coeff_imag * value_real
    return (out_real, out_imag)

def apply_adjoint(link_pair, field_pair):
    link_real, link_imag = link_pair
    field_real, field_imag = field_pair
    out_real = 0.0
    out_imag = 0.0
    for column in range(3):
        coeff_real = link_real[column][None]
        coeff_imag = link_imag[column][None]
        value_real = field_real[:, column][:, None]
        value_imag = field_imag[:, column][:, None]
        out_real = out_real + coeff_real * value_real + coeff_imag * value_imag
        out_imag = out_imag + coeff_real * value_imag - coeff_imag * value_real
    return (out_real, out_imag)

def covariant(up_pair, down_pair, ahead_pair, behind_pair):
    forward = apply_link(up_pair, ahead_pair)
    backward = apply_adjoint(down_pair, behind_pair)
    return (0.5 * (forward[0] - backward[0]), 0.5 * (forward[1] - backward[1]))

def phase_table(momentum, x_coords, y_coords, z_coords, extent_x, extent_y, extent_z):
    frac_x = (momentum[0] * x_coords % extent_x).astype(jnp.float32) / extent_x
    frac_y = (momentum[1] * y_coords % extent_y).astype(jnp.float32) / extent_y
    frac_z = (momentum[2] * z_coords % extent_z).astype(jnp.float32) / extent_z
    summed = frac_z[:, None, None] + frac_y[None, :, None] + frac_x[None, None, :]
    angle = 2.0 * math.pi * summed
    return (jnp.cos(angle), jnp.sin(angle))

def make_operators(field_pair, ahead_list, behind_list, up_list, down_list, directions, cosine, sine):
    derived = [covariant(up_list[axis_number], down_list[axis_number], ahead_list[axis_number], behind_list[axis_number]) for axis_number in range(3)]
    results = []
    for op_slot in range(3):
        chosen = directions[op_slot]
        real_part = jnp.where(chosen == 0, derived[0][0], jnp.where(chosen == 1, derived[1][0], derived[2][0]))
        imag_part = jnp.where(chosen == 0, derived[0][1], jnp.where(chosen == 1, derived[1][1], derived[2][1]))
        results.append(jnp.stack([real_part, imag_part], -2).astype(jnp.bfloat16))
    field_real, field_imag = field_pair
    phased_real = field_real * cosine + field_imag * sine
    phased_imag = field_imag * cosine - field_real * sine
    results.append(jnp.stack([phased_real, phased_imag], -2).astype(jnp.bfloat16))
    return jnp.stack(results, 1)

def contract(rows, stacked_left):
    row_count = rows.shape[0]
    flat_rows = rows.reshape(row_count * 4, -1)
    product = lax.dot_general(flat_rows, stacked_left, (((1,), (1,)), ((), ())), preferred_element_type=jnp.float32)
    return product.reshape(row_count, 4, 2, stacked_left.shape[0] // 2)

def reference(vectors, links, momentum, directions):
    six_dims = vectors.reshape(NEV, 3, NZ, NY, 2, LX)
    swapped = jnp.stack([-six_dims[..., 1, :], six_dims[..., 0, :]], -2)
    stacked_left = jnp.concatenate([vectors.reshape(NEV, -1), swapped.reshape(NEV, -1)], 0)
    link_wide = links.astype(jnp.float32).reshape(3, 3, 3, NZ, NY, 2, LX)
    up_list = [(link_wide[axis_number, ..., 0, :], link_wide[axis_number, ..., 1, :]) for axis_number in range(3)]
    down_list = [(jnp.roll(up_list[axis_number][0], 1, axis=-1 - axis_number), jnp.roll(up_list[axis_number][1], 1, axis=-1 - axis_number)) for axis_number in range(3)]
    cosine, sine = phase_table(momentum, jnp.arange(LX, dtype=jnp.int32), jnp.arange(NY, dtype=jnp.int32), jnp.arange(NZ, dtype=jnp.int32), LX, NY, NZ)
    block_size = NEV // 16

    def one_block(block_index):
        first_row = (block_index * block_size).astype(jnp.int32)
        block = lax.dynamic_slice_in_dim(vectors, first_row, block_size, 0)
        widened = block.astype(jnp.float32).reshape(block_size, 3, NZ, NY, 2, LX)
        field_real = widened[..., 0, :]
        field_imag = widened[..., 1, :]
        ahead_list = [(jnp.roll(field_real, -1, axis=-1 - axis_number), jnp.roll(field_imag, -1, axis=-1 - axis_number)) for axis_number in range(3)]
        behind_list = [(jnp.roll(field_real, 1, axis=-1 - axis_number), jnp.roll(field_imag, 1, axis=-1 - axis_number)) for axis_number in range(3)]
        transformed = make_operators((field_real, field_imag), ahead_list, behind_list, up_list, down_list, directions, cosine, sine)
        return contract(transformed.reshape(block_size, 4, -1), stacked_left)
    blocks = lax.map(one_block, jnp.arange(16, dtype=jnp.int32))
    summed = blocks.reshape(NEV, 4, 2, NEV) * (1.0 / math.sqrt(LX * NY * NZ))
    return jnp.transpose(summed, (1, 2, 0, 3))
```

```python
import functools
import math

import jax
import jax.numpy as jnp
from jax import lax
from jax.experimental import pallas as pl
from jax.experimental.pallas import tpu as pltpu
from jax.sharding import PartitionSpec as P

F32 = jnp.float32
BF16 = jnp.bfloat16
VMEM = pl.BlockSpec(memory_space=pltpu.VMEM)
SMEM = pl.BlockSpec(memory_space=pltpu.SMEM)

NV = 64
COL = 3
DZ = 8
HY = 2
LANES = 128
HALF = 64
NZY = DZ * HY
NK = COL * NZY
KDIM = NK * LANES


def params(limit):
    return pltpu.CompilerParams(vmem_limit_bytes=limit * 1024 * 1024)


def shape(dims, dtype):
    return jax.ShapeDtypeStruct(dims, dtype)


def prepare_kernel(v_ref, l_ref, vt_ref, y0_ref, y1_ref, z0_ref, z1_ref, wide, lwide):
    wide[...] = v_ref[...].astype(F32)
    lwide[0:432, :] = l_ref[...].astype(F32)
    lwide[432:576, :] = jnp.zeros((144, LANES), F32)
    for k in range(NK):
        tile = wide[pl.ds(k, NV, stride=NK), :].astype(BF16)
        c, z, y = k // NZY, (k % NZY) // HY, k % HY
        vt_ref[k] = tile
        if y == 0:
            y0_ref[c * DZ + z] = tile
        else:
            y1_ref[c * DZ + z] = tile
        if z == 0:
            z0_ref[c * HY + y] = tile
        if z == DZ - 1:
            z1_ref[c * HY + y] = tile
    rim = lwide[pl.ds(9 * NZY + 1, 72, stride=HY), :]
    rim = jnp.concatenate([rim, jnp.zeros((56, LANES), F32)], 0).astype(BF16)
    y1_ref[24] = rim[0:64]
    y1_ref[25] = rim[64:128]
    low = lwide[pl.ds(18 * NZY + 14, 16, stride=NZY), :]
    high = lwide[pl.ds(18 * NZY + 15, 16, stride=NZY), :]
    rest = jnp.zeros((32, LANES), F32)
    z1_ref[6] = jnp.concatenate([low, high, rest], 0).astype(BF16)


def prepare(rows, link_rows):
    return pl.pallas_call(
        prepare_kernel,
        out_shape=(
            shape((NK, NV, LANES), BF16),
            shape((24, NV, LANES), BF16),
            shape((26, NV, LANES), BF16),
            shape((6, NV, LANES), BF16),
            shape((7, NV, LANES), BF16),
        ),
        in_specs=[VMEM] * 2,
        out_specs=(VMEM,) * 5,
        scratch_shapes=[pltpu.VMEM((NV * NK, LANES), F32), pltpu.VMEM((576, LANES), F32)],
        compiler_params=params(16),
        cost_estimate=pl.CostEstimate(flops=0, bytes_accessed=3000000, transcendentals=0),
        name="prepare",
    )(rows, link_rows)


def stencil_kernel(
    dirs_ref, vt_ref, yp_ref, ym_ref, zp_ref, zm_ref, l_ref, cos_ref, sin_ref, w_ref,
    ext, exts, lwide, real, imag, upr, upi, dnr, dni,
):
    lane = lax.broadcasted_iota(jnp.int32, (1, LANES), 1)
    first = lane < HALF
    sign = jnp.where(first, -1.0, 1.0).astype(F32)

    def put(c, z, y, tile):
        wide = tile.astype(F32)
        ext[c, z, y] = wide
        exts[c, z, y] = pltpu.roll(wide, HALF, 1)

    for c in range(COL):
        for z in range(DZ):
            for y in range(HY):
                put(c, z + 1, y + 1, vt_ref[(c * DZ + z) * HY + y])
            put(c, z + 1, HY + 1, yp_ref[c * DZ + z])
            put(c, z + 1, 0, ym_ref[c * DZ + z])
        for y in range(HY):
            put(c, DZ + 1, y + 1, zp_ref[c * HY + y])
            put(c, 0, y + 1, zm_ref[c * HY + y])

    def coefficients(rows):
        half = rows * 0.5
        swapped = pltpu.roll(half, HALF, 1)
        return jnp.where(first, half, swapped), jnp.where(first, swapped, half)

    lwide[0:432, :] = l_ref[...].astype(F32)
    lwide[432:504, :] = jnp.concatenate([ym_ref[24], ym_ref[25]], 0).astype(F32)[0:72]
    zrim = zm_ref[6].astype(F32)
    lwide[504:520, :] = zrim[0:16]
    lwide[520:536, :] = zrim[16:32]
    re, im = coefficients(lwide[...])
    real[...] = re
    imag[...] = im
    for zy in range(NZY):
        z, y = zy // HY, zy % HY
        pick = pl.ds(zy, 27, stride=NZY)
        upr[zy, 0:27, :] = real[pick, :]
        upi[zy, 0:27, :] = imag[pick, :] * sign
        pick = pl.ds(zy, 9, stride=NZY)
        dnr[zy, 0:9, :] = pltpu.roll(real[pick, :], 1, 1)
        dni[zy, 0:9, :] = pltpu.roll(imag[pick, :], 1, 1) * sign
        pick = pl.ds(432 + z, 9, stride=DZ) if y == 0 else pl.ds(9 * NZY + zy - 1, 9, stride=NZY)
        dnr[zy, 9:18, :] = real[pick, :]
        dni[zy, 9:18, :] = imag[pick, :] * sign
        pick = pl.ds(504 + 16 * y, 9) if z == 0 else pl.ds(18 * NZY + zy - HY, 9, stride=NZY)
        dnr[zy, 18:27, :] = real[pick, :]
        dni[zy, 18:27, :] = imag[pick, :] * sign

    slots = [
        sum(jnp.where(dirs_ref[o] == mu, o, 0) for o in range(3)).astype(jnp.int32)
        for mu in range(3)
    ]
    wrap_up = (lane == HALF - 1) | (lane == LANES - 1)
    wrap_down = (lane == 0) | (lane == HALF)

    def site(zy, carry):
        z = lax.div(zy, HY) + 1
        y = lax.rem(zy, HY) + 1
        def neighbour(mu, c, step):
            if mu == 1:
                return ext[c, z, y + step], exts[c, z, y + step]
            if mu == 2:
                return ext[c, z + step, y], exts[c, z + step, y]
            here, swap = ext[c, z, y], exts[c, z, y]
            a = pltpu.roll(here, (-step) % LANES, 1)
            b = pltpu.roll(swap, (-step) % LANES, 1)
            wrap = wrap_up if step == 1 else wrap_down
            return jnp.where(wrap, b, a), jnp.where(wrap, a, b)

        for mu in range(3):
            out = [None] * 3
            for c in range(COL):
                here, swap = neighbour(mu, c, 1)
                for r in range(3):
                    at = mu * 9 + r * 3 + c
                    term = here * upr[zy, at:at + 1, :] + swap * upi[zy, at:at + 1, :]
                    out[r] = term if out[r] is None else out[r] + term
            for c in range(COL):
                here, swap = neighbour(mu, c, -1)
                for r in range(3):
                    at = mu * 9 + c * 3 + r
                    term = here * dnr[zy, at:at + 1, :] - swap * dni[zy, at:at + 1, :]
                    out[r] = out[r] - term
            for r in range(3):
                column = pl.multiple_of((r * NZY + zy) * LANES, LANES)
                w_ref[slots[mu], :, pl.ds(column, LANES)] = out[r].astype(BF16)
        cosine = cos_ref[pl.ds(zy, 1), :]
        sine = sin_ref[pl.ds(zy, 1), :]
        for c in range(COL):
            column = pl.multiple_of((c * NZY + zy) * LANES, LANES)
            phased = ext[c, z, y] * cosine + exts[c, z, y] * sine
            w_ref[3, :, pl.ds(column, LANES)] = phased.astype(BF16)
        return carry

    lax.fori_loop(0, NZY, site, 0)


def stencil(directions, vt, yp, ym, zp, zm, link_rows, cosine, sine):
    table = pltpu.VMEM((NZY, 32, LANES), F32)
    return pl.pallas_call(
        stencil_kernel,
        out_shape=shape((4, NV, KDIM), BF16),
        in_specs=[SMEM] + [VMEM] * 8,
        out_specs=VMEM,
        scratch_shapes=[
            pltpu.VMEM((COL, DZ + 2, HY + 2, NV, LANES), F32),
            pltpu.VMEM((COL, DZ + 2, HY + 2, NV, LANES), F32),
            pltpu.VMEM((536, LANES), F32),
            pltpu.VMEM((536, LANES), F32),
            pltpu.VMEM((536, LANES), F32),
            table,
            table,
            table,
            table,
        ],
        compiler_params=params(24),
        cost_estimate=pl.CostEstimate(flops=60000000, bytes_accessed=6000000, transcendentals=0),
        name="stencil",
    )(directions, vt, yp, ym, zp, zm, link_rows, cosine, sine)


def contract_kernel(counts, core_ref, w_ref, *refs):
    blocks = refs[: len(counts)]
    keep_ref, send_ref, wide, right, product = refs[len(counts):]
    total = sum(counts)
    lane = lax.broadcasted_iota(jnp.int32, (1, LANES), 1)
    sign = jnp.where(lane < HALF, -1.0, 1.0).astype(F32)
    start = 0
    for block, count in zip(blocks, counts):
        wide[0:count * NK, :] = block[...].astype(F32)
        for k in range(NK):
            tile = wide[pl.ds(k, count, stride=NK), :]
            swap = pltpu.roll(tile, HALF, 1) * sign
            right[start:start + count, k * LANES:(k + 1) * LANES] = tile.astype(BF16)
            right[total + start:total + start + count, k * LANES:(k + 1) * LANES] = swap.astype(BF16)
        start += count
    left = w_ref[...].reshape(4 * NV, KDIM)
    dots = lax.dot_general(left, right[...], (((1,), (1,)), ((), ())), preferred_element_type=F32)
    product[...] = dots.reshape(2, 2 * NV, 2 * total)
    mine = core_ref[0]
    keep_ref[...] = product[mine]
    send_ref[...] = product[1 - mine]


def contract(core, w, blocks):
    counts = tuple(b.shape[0] // NK for b in blocks)
    total = sum(counts)
    out = shape((2 * NV, 2 * total), F32)
    return pl.pallas_call(
        functools.partial(contract_kernel, counts),
        out_shape=(out, out),
        in_specs=[SMEM] + [VMEM] * (1 + len(blocks)),
        out_specs=(VMEM, VMEM),
        scratch_shapes=[
            pltpu.VMEM((NV * NK, LANES), F32),
            pltpu.VMEM((2 * total, KDIM), BF16),
            pltpu.VMEM((2, 2 * NV, 2 * total), F32),
        ],
        compiler_params=params(32),
        cost_estimate=pl.CostEstimate(
            flops=2 * 256 * 2 * total * KDIM, bytes_accessed=4000000, transcendentals=0
        ),
        name="contract",
    )(core, w, *blocks)


def finish_kernel(scale, where_ref, a0_ref, a1_ref, b0_ref, b1_ref, out_ref):
    shift, core = where_ref[0], where_ref[1]
    a = [a0_ref[...], a1_ref[...]]
    b = [b0_ref[...], b1_ref[...]]
    for ch in range(2):
        for part in range(2):
            near = a[ch][:, part * 192:(part + 1) * 192]
            far = b[ch][:, part * 64:(part + 1) * 64]
            line = jnp.concatenate([near[:, 0:128], far, near[:, 128:192]], 1) * scale
            line = pltpu.roll(line, shift, 1)
            at = 2 * (core if ch == 0 else 1 - core)
            out_ref[at, part] = line[0:NV]
            out_ref[at + 1, part] = line[NV:2 * NV]


def finish(where, near_mine, near_other, far_mine, far_other, scale):
    return pl.pallas_call(
        functools.partial(finish_kernel, scale),
        out_shape=shape((4, 2, NV, 256), F32),
        in_specs=[SMEM] + [VMEM] * 4,
        out_specs=VMEM,
        compiler_params=params(16),
        cost_estimate=pl.CostEstimate(flops=200000, bytes_accessed=1000000, transcendentals=0),
        name="finish",
    )(where, near_mine, near_other, far_mine, far_other)


def permuted(value, axis, target):
    size = lax.axis_size(axis)
    return lax.ppermute(value, axis, [(source, target(source)) for source in range(size)])


def four_sum(own, axis_opposite, axis_side, axis_other):
    wide = [t.astype(F32) for t in (own, axis_opposite, axis_side, axis_other)]
    return (wide[0] + wide[1]) + (wide[2] + wide[3])


def body(vectors, links, momentum, directions):
    vec = lax.axis_index("vec")
    rows = vectors.reshape(NV * NK, LANES)
    link_rows = links.reshape(27 * NZY, LANES)
    mid = NV * NK // 2
    ring_up = lambda v: permuted(v, "vec", lambda s: (s + 1) % 4)
    ring_down = lambda v: permuted(v, "vec", lambda s: (s - 1) % 4)
    low, high = rows[:mid], rows[mid:]
    prev_low = ring_up(low)
    next_high = ring_down(high)
    prev_high = ring_up(high)
    next_low = ring_down(low)
    far_low = ring_up(prev_low)
    far_high = ring_down(next_high)

    vt, y0, y1, z0, z1 = prepare(rows, link_rows)
    yp = permuted(y0, "gy", lambda s: (s - 1) % 8)
    ym = permuted(y1, "gy", lambda s: (s + 1) % 8)
    zp = permuted(z0, "gz", lambda s: (s - 1) % 4)
    zm = permuted(z1, "gz", lambda s: (s + 1) % 4)

    width, extent_y, extent_z = HALF, 16, 32
    x = jnp.arange(LANES, dtype=jnp.int32) % HALF
    zy = jnp.arange(NZY, dtype=jnp.int32)
    y = lax.axis_index("gy") * HY + zy % HY
    z = lax.axis_index("gz") * DZ + zy // HY
    frac_x = (momentum[0] * x % width).astype(F32) / width
    frac_y = (momentum[1] * y % extent_y).astype(F32) / extent_y
    frac_z = (momentum[2] * z % extent_z).astype(F32) / extent_z
    angle = 2.0 * math.pi * ((frac_z + frac_y)[:, None] + frac_x[None, :])
    cosine = jnp.cos(angle)
    sine = jnp.sin(angle) * jnp.where(jnp.arange(LANES) < HALF, 1.0, -1.0).astype(F32)

    w = stencil(directions, vt, yp, ym, zp, zm, link_rows, cosine, sine)

    core = lax.axis_index("gz") % 2
    core_ref = core.reshape(1).astype(jnp.int32)
    near_keep, near_send = contract(core_ref, w, [rows, next_low, next_high, prev_low, prev_high])
    far_keep, far_send = contract(core_ref, w, [far_low, far_high])

    mate = lambda v: permuted(v, "gz", lambda s: s ^ 1)
    along_x = lambda v, step: permuted(v, "gy", lambda s: (s // 4) * 4 + (s + step) % 4)

    def summed(keep, send):
        chip = (keep + mate(send)).astype(BF16)
        row = four_sum(chip, along_x(chip, 2), along_x(chip, 1), along_x(chip, 3)).astype(BF16)
        far = permuted(row, "gy", lambda s: s ^ 4)
        side = permuted(row, "gz", lambda s: s ^ 2)
        both = permuted(row, ("gz", "gy"), lambda s: s ^ 20)
        plane = four_sum(row, far, side, both)
        return plane, mate(plane)

    near, near_other = summed(near_keep, near_send)
    far, far_other = summed(far_keep, far_send)
    where = jnp.stack([vec * HALF, core]).astype(jnp.int32)
    scale = 1.0 / math.sqrt(width * extent_y * extent_z)
    return finish(where, near, near_other, far, far_other, scale)


def solution(mesh):
    in_specs = (P("vec", None, "gz", "gy", None), P(None, None, None, "gz", "gy", None), P(), P())
    out_specs = P(None, None, "vec", None)
    return jax.shard_map(body, mesh=mesh, in_specs=in_specs, out_specs=out_specs, check_vma=False)
```

```python
import functools
import math

import jax
import jax.numpy as jnp
from jax import lax
from jax.experimental import pallas as pl
from jax.experimental.pallas import tpu as pltpu
from jax.sharding import PartitionSpec as P

F32 = jnp.float32
BF16 = jnp.bfloat16
VMEM = pl.BlockSpec(memory_space=pltpu.VMEM)
SMEM = pl.BlockSpec(memory_space=pltpu.SMEM)
ANY = pl.BlockSpec(memory_space=pl.ANY)
HBM = pl.BlockSpec(memory_space=pltpu.HBM)

NV = 64
COL = 3
DZ = 8
HY = 2
LANES = 128
HALF = 64
NZY = DZ * HY
EXT_X, EXT_Y, EXT_Z = 64, 16, 32
NK = COL * NZY
KDIM = NK * LANES


def params(limit):
    return pltpu.CompilerParams(vmem_limit_bytes=limit * 1024 * 1024)


def shape(dims, dtype):
    return jax.ShapeDtypeStruct(dims, dtype)


def fetch(sources, targets, sem):
    copies = [
        pltpu.make_async_copy(source, target, sem.at[i])
        for i, (source, target) in enumerate(zip(sources, targets))
    ]
    for copy in copies:
        copy.start()
    return copies


def prepare_kernel(rows, lrows, y0_ref, y1_ref, z0_ref, z1_ref, wide, lwide):
    wide[...] = rows[...].astype(F32)
    lwide[0:432, :] = lrows[...].astype(F32)
    lwide[432:576, :] = jnp.zeros((144, LANES), F32)
    for k in range(NK):
        tile = wide[pl.ds(k, NV, stride=NK), :].astype(BF16)
        c, z, y = k // NZY, (k % NZY) // HY, k % HY
        if y == 0:
            y0_ref[c * DZ + z] = tile
        else:
            y1_ref[c * DZ + z] = tile
        if z == 0:
            z0_ref[c * HY + y] = tile
        if z == DZ - 1:
            z1_ref[c * HY + y] = tile
    rim = lwide[pl.ds(9 * NZY + 1, 72, stride=HY), :]
    rim = jnp.concatenate([rim, jnp.zeros((56, LANES), F32)], 0).astype(BF16)
    y1_ref[24] = rim[0:64]
    y1_ref[25] = rim[64:128]
    low = lwide[pl.ds(18 * NZY + 14, 16, stride=NZY), :]
    high = lwide[pl.ds(18 * NZY + 15, 16, stride=NZY), :]
    rest = jnp.zeros((32, LANES), F32)
    z1_ref[6] = jnp.concatenate([low, high, rest], 0).astype(BF16)


def prepare(rows, link_rows):
    return pl.pallas_call(
        prepare_kernel,
        out_shape=(
            shape((24, NV, LANES), BF16),
            shape((26, NV, LANES), BF16),
            shape((6, NV, LANES), BF16),
            shape((7, NV, LANES), BF16),
        ),
        in_specs=[VMEM] * 2,
        out_specs=(VMEM,) * 4,
        scratch_shapes=[
            pltpu.VMEM((NV * NK, LANES), F32),
            pltpu.VMEM((576, LANES), F32),
        ],
        compiler_params=params(6),
        cost_estimate=pl.CostEstimate(flops=2000000000, bytes_accessed=3000000, transcendentals=0),
        name="prepare",
    )(rows, link_rows)


def line_coefficients(rows, first):
    half = rows * 0.5
    swapped = pltpu.roll(half, HALF, 1)
    return jnp.where(first, half, swapped), jnp.where(first, swapped, half)


def lane_masks():
    lane = lax.broadcasted_iota(jnp.int32, (1, LANES), 1)
    return lane, lane < HALF, jnp.where(lane < HALF, -1.0, 1.0).astype(F32)


def derivative(mu, neighbour, tables, zy, store):
    upr, upi, dnr, dni = tables
    out = [None] * 3
    for c in range(COL):
        here, swap = neighbour(c, 1)
        for r in range(3):
            at = mu * 9 + r * 3 + c
            term = here * upr[zy, at:at + 1, :] + swap * upi[zy, at:at + 1, :]
            out[r] = term if out[r] is None else out[r] + term
    for c in range(COL):
        here, swap = neighbour(c, -1)
        for r in range(3):
            at = mu * 9 + c * 3 + r
            term = here * dnr[zy, at:at + 1, :] - swap * dni[zy, at:at + 1, :]
            out[r] = out[r] - term
    for r in range(3):
        store(r, out[r].astype(BF16))


def local_kernel(
    momentum_ref, v_ref, l_ref, w_ref, ext, exts, upr, upi, dnr, dni,
    wide, lwide, real, imag, cos_ref, sin_ref,
):
    lane, first, sign = lane_masks()
    at = lax.broadcasted_iota(jnp.int32, (NZY, LANES), 0)
    x = lax.broadcasted_iota(jnp.int32, (NZY, LANES), 1) & (HALF - 1)
    y = lax.axis_index("gy").astype(jnp.int32) * HY + (at & (HY - 1))
    z = lax.axis_index("gz").astype(jnp.int32) * DZ + (at >> 1)
    frac_x = ((momentum_ref[0] * x) & (EXT_X - 1)).astype(F32) / EXT_X
    frac_y = ((momentum_ref[1] * y) & (EXT_Y - 1)).astype(F32) / EXT_Y
    frac_z = ((momentum_ref[2] * z) & (EXT_Z - 1)).astype(F32) / EXT_Z
    angle = 2.0 * math.pi * (frac_z + frac_y + frac_x)
    cos_ref[...] = jnp.cos(angle)
    sin_ref[...] = -sign * jnp.sin(angle)

    wide[...] = v_ref[...].astype(F32)
    for c in range(COL):
        for z in range(DZ):
            for y in range(HY):
                tile = wide[pl.ds((c * DZ + z) * HY + y, NV, stride=NK), :]
                ext[c, z + 1, y + 1] = tile
                exts[c, z + 1, y + 1] = pltpu.roll(tile, HALF, 1)

    lwide[...] = l_ref[...].astype(F32)
    re, im = line_coefficients(lwide[...], first)
    real[...] = re
    imag[...] = im
    for zy in range(NZY):
        z, y = zy // HY, zy % HY
        pick = pl.ds(zy, 27, stride=NZY)
        upr[zy, 0:27, :] = real[pick, :]
        upi[zy, 0:27, :] = imag[pick, :] * sign
        pick = pl.ds(zy, 9, stride=NZY)
        dnr[zy, 0:9, :] = pltpu.roll(real[pick, :], 1, 1)
        dni[zy, 0:9, :] = pltpu.roll(imag[pick, :], 1, 1) * sign
        if y:
            pick = pl.ds(9 * NZY + zy - 1, 9, stride=NZY)
            dnr[zy, 9:18, :] = real[pick, :]
            dni[zy, 9:18, :] = imag[pick, :] * sign
        if z:
            pick = pl.ds(18 * NZY + zy - HY, 9, stride=NZY)
            dnr[zy, 18:27, :] = real[pick, :]
            dni[zy, 18:27, :] = imag[pick, :] * sign

    wrap_up = (lane == HALF - 1) | (lane == LANES - 1)
    wrap_down = (lane == 0) | (lane == HALF)

    def site(zy, carry):
        z = lax.div(zy, HY) + 1
        y = lax.rem(zy, HY) + 1

        def neighbour(c, step):
            here, swap = ext[c, z, y], exts[c, z, y]
            a = pltpu.roll(here, (-step) % LANES, 1)
            b = pltpu.roll(swap, (-step) % LANES, 1)
            wrap = wrap_up if step == 1 else wrap_down
            return jnp.where(wrap, b, a), jnp.where(wrap, a, b)

        def store(r, value):
            column = pl.multiple_of((r * NZY + zy) * LANES, LANES)
            w_ref[0, :, pl.ds(column, LANES)] = value

        derivative(0, neighbour, (upr, upi, dnr, dni), zy, store)
        cosine = cos_ref[pl.ds(zy, 1), :]
        sine = sin_ref[pl.ds(zy, 1), :]
        for c in range(COL):
            column = pl.multiple_of((c * NZY + zy) * LANES, LANES)
            phased = ext[c, z, y] * cosine + exts[c, z, y] * sine
            w_ref[1, :, pl.ds(column, LANES)] = phased.astype(BF16)
        return carry

    lax.fori_loop(0, NZY, site, 0)


EXTENDED = (COL, DZ + 2, HY + 2, NV, LANES)
TABLE = (NZY, 32, LANES)


def local_terms(momentum, rows, link_rows):
    line = pltpu.VMEM((27 * NZY, LANES), F32)
    return pl.pallas_call(
        local_kernel,
        out_shape=(shape((4, NV, KDIM), BF16),)
        + (shape(EXTENDED, F32),) * 2
        + (shape(TABLE, F32),) * 4,
        in_specs=[SMEM] + [VMEM] * 2,
        out_specs=(VMEM,) * 7,
        scratch_shapes=[
            pltpu.VMEM((NV * NK, LANES), F32),
            line,
            line,
            line,
            pltpu.VMEM((NZY, LANES), F32),
            pltpu.VMEM((NZY, LANES), F32),
        ],
        compiler_params=params(8),
        cost_estimate=pl.CostEstimate(flops=6000000000, bytes_accessed=6000000, transcendentals=0),
        name="local_terms",
    )(momentum, rows, link_rows)


def border_kernel(
    local_ref, e_ref, s_ref, upr, upi, r_ref, i_ref, yp_ref, ym_ref, zp_ref, zm_ref,
    w_ref, ext, exts, dnr, dni, lwide, real, imag,
):
    lane, first, sign = lane_masks()

    def put(c, z, y, tile):
        tile = tile.astype(F32)
        ext[c, z, y] = tile
        exts[c, z, y] = pltpu.roll(tile, HALF, 1)

    for c in range(COL):
        for z in range(DZ):
            put(c, z + 1, HY + 1, yp_ref[c * DZ + z])
            put(c, z + 1, 0, ym_ref[c * DZ + z])
        for y in range(HY):
            put(c, DZ + 1, y + 1, zp_ref[c * HY + y])
            put(c, 0, y + 1, zm_ref[c * HY + y])

    lwide[0:128, :] = jnp.concatenate([ym_ref[24], ym_ref[25]], 0).astype(F32)
    lwide[128:192, :] = zm_ref[6].astype(F32)
    re, im = line_coefficients(lwide[...], first)
    real[...] = re
    imag[...] = im * sign
    for z in range(DZ):
        pick = pl.ds(z, 9, stride=DZ)
        dnr[z * HY, 9:18, :] = real[pick, :]
        dni[z * HY, 9:18, :] = imag[pick, :]
    for y in range(HY):
        pick = pl.ds(128 + 16 * y, 9)
        dnr[y, 18:27, :] = real[pick, :]
        dni[y, 18:27, :] = imag[pick, :]

    def site(zy, carry):
        z = lax.div(zy, HY) + 1
        y = lax.rem(zy, HY) + 1
        for mu in (1, 2):

            def neighbour(c, step):
                at = (c, z, y + step) if mu == 1 else (c, z + step, y)
                return ext[at], exts[at]

            def store(r, value):
                column = pl.multiple_of((r * NZY + zy) * LANES, LANES)
                w_ref[mu + 1, :, pl.ds(column, LANES)] = value

            derivative(mu, neighbour, (upr, upi, dnr, dni), zy, store)
        return carry

    lax.fori_loop(0, NZY, site, 0)


def border_terms(w, ext, exts, upr, upi, dnr, dni, yp, ym, zp, zm):
    line = pltpu.VMEM((192, LANES), F32)
    return pl.pallas_call(
        border_kernel,
        out_shape=(shape((4, NV, KDIM), BF16),)
        + (shape(EXTENDED, F32),) * 2
        + (shape(TABLE, F32),) * 2,
        in_specs=[VMEM] * 11,
        out_specs=(VMEM,) * 5,
        input_output_aliases={0: 0, 1: 1, 2: 2, 5: 3, 6: 4},
        scratch_shapes=[line, line, line],
        compiler_params=params(4),
        cost_estimate=pl.CostEstimate(flops=6000000000, bytes_accessed=6000000, transcendentals=0),
        name="border_terms",
    )(w, ext, exts, upr, upi, dnr, dni, yp, ym, zp, zm)[0]


def fill_right(counts, blocks, wide, right):
    total = sum(counts)
    lane, first, sign = lane_masks()
    start = 0
    for block, count in zip(blocks, counts):
        wide[0:count * NK, :] = block[...].astype(F32)
        for k in range(NK):
            tile = wide[pl.ds(k, count, stride=NK), :]
            swap = pltpu.roll(tile, HALF, 1) * sign
            right[start:start + count, k * LANES:(k + 1) * LANES] = tile.astype(BF16)
            right[total + start:total + start + count, k * LANES:(k + 1) * LANES] = swap.astype(BF16)
        start += count


def dot_halves(w_ref, right, keep_ref, send_ref, product):
    left = w_ref[...].reshape(4 * NV, KDIM)
    dots = lax.dot_general(left, right[...], (((1,), (1,)), ((), ())), preferred_element_type=F32)
    product[...] = dots.reshape(2, 2 * NV, dots.shape[1])
    mine = lax.axis_index("gz").astype(jnp.int32) & 1
    keep_ref[...] = product[mine]
    send_ref[...] = product[1 - mine]


def right_kernel(counts, *refs):
    n = len(counts)
    fill_right(counts, refs[:n], refs[n + 1], refs[n])


def right_side(blocks):
    counts = tuple(b.shape[0] // NK for b in blocks)
    return pl.pallas_call(
        functools.partial(right_kernel, counts),
        out_shape=shape((2 * sum(counts), KDIM), BF16),
        in_specs=[VMEM] * len(blocks),
        out_specs=VMEM,
        scratch_shapes=[pltpu.VMEM((max(counts) * NK, LANES), F32)],
        compiler_params=params(4),
        cost_estimate=pl.CostEstimate(flops=2000000000, bytes_accessed=4000000, transcendentals=0),
        name="right_side",
    )(*blocks)


def near_kernel(w_ref, right_ref, keep_ref, send_ref, product):
    dot_halves(w_ref, right_ref, keep_ref, send_ref, product)


def far_kernel(counts, w_ref, *refs):
    n = len(counts)
    keep_ref, send_ref, wide, right, product = refs[n:]
    fill_right(counts, refs[:n], wide, right)
    dot_halves(w_ref, right, keep_ref, send_ref, product)


def contract_near(w, right):
    columns = right.shape[0]
    out = shape((2 * NV, columns), F32)
    return pl.pallas_call(
        near_kernel,
        out_shape=(out, out),
        in_specs=[VMEM] * 2,
        out_specs=(VMEM, VMEM),
        scratch_shapes=[pltpu.VMEM((2, 2 * NV, columns), F32)],
        compiler_params=params(4),
        cost_estimate=pl.CostEstimate(
            flops=2 * 256 * columns * KDIM, bytes_accessed=4000000, transcendentals=0
        ),
        name="contract_near",
    )(w, right)


def contract_far(w, blocks):
    counts = tuple(b.shape[0] // NK for b in blocks)
    columns = 2 * sum(counts)
    out = shape((2 * NV, columns), F32)
    return pl.pallas_call(
        functools.partial(far_kernel, counts),
        out_shape=(out, out),
        in_specs=[VMEM] * (1 + len(blocks)),
        out_specs=(VMEM, VMEM),
        scratch_shapes=[
            pltpu.VMEM((max(counts) * NK, LANES), F32),
            pltpu.VMEM((columns, KDIM), BF16),
            pltpu.VMEM((2, 2 * NV, columns), F32),
        ],
        compiler_params=params(5),
        cost_estimate=pl.CostEstimate(
            flops=2 * 256 * columns * KDIM, bytes_accessed=4000000, transcendentals=0
        ),
        name="contract_far",
    )(w, *blocks)


def finish_kernel(scale, dirs_ref, mine_ref, other_ref, out_ref):
    shift = lax.axis_index("vec").astype(jnp.int32) * HALF
    core = lax.axis_index("gz").astype(jnp.int32) & 1
    slots = [
        sum(jnp.where(dirs_ref[o] == mu, o, 0) for o in range(3)).astype(jnp.int32)
        for mu in range(3)
    ]
    for ch, rows_ref in enumerate((mine_ref, other_ref)):
        rows = rows_ref[...]
        for part in range(2):
            near = rows[:, part * 192:(part + 1) * 192]
            far = rows[:, 384 + part * 64:384 + (part + 1) * 64]
            line = jnp.concatenate([near[:, 0:128], far, near[:, 128:192]], 1) * scale
            line = pltpu.roll(line, shift, 1)
            half = core if ch == 0 else 1 - core
            out_ref[jnp.where(half == 0, slots[0], slots[1]), part] = line[0:NV]
            out_ref[jnp.where(half == 0, 3, slots[2]), part] = line[NV:2 * NV]


def finish(directions, mine, other, scale):
    return pl.pallas_call(
        functools.partial(finish_kernel, scale),
        out_shape=shape((4, 2, NV, 256), F32),
        in_specs=[SMEM] + [VMEM] * 2,
        out_specs=VMEM,
        compiler_params=params(16),
        cost_estimate=pl.CostEstimate(flops=200000, bytes_accessed=1000000, transcendentals=0),
        name="finish",
    )(directions, mine, other)


def permuted(value, axis, target):
    size = lax.axis_size(axis)
    return lax.ppermute(value, axis, [(source, target(source)) for source in range(size)])


def four_sum(own, axis_opposite, axis_side, axis_other):
    wide = [t.astype(F32) for t in (own, axis_opposite, axis_side, axis_other)]
    return (wide[0] + wide[1]) + (wide[2] + wide[3])


def body(vectors, links, momentum, directions):
    rows = vectors.reshape(NV * NK, LANES)
    link_rows = links.reshape(27 * NZY, LANES)
    mid = NV * NK // 2
    prev = permuted(rows, "vec", lambda s: (s + 1) % 4)
    next_ = permuted(rows, "vec", lambda s: (s - 1) % 4)

    y0, y1, z0, z1 = prepare(rows, link_rows)
    yp = permuted(y0, "gy", lambda s: (s - 1) % 8)
    ym = permuted(y1, "gy", lambda s: (s + 1) % 8)
    prev, next_, zz = lax.optimization_barrier((prev, next_, z1))
    zp = permuted(z0, "gz", lambda s: (s - 1) % 4)
    z1, zp = lax.optimization_barrier((zz, zp))
    zm = permuted(z1, "gz", lambda s: (s + 1) % 4)
    partial = local_terms(momentum, rows, link_rows)

    far_low = permuted(prev[:mid], "vec", lambda s: (s + 1) % 4)
    far_high = permuted(next_[mid:], "vec", lambda s: (s - 1) % 4)

    right = right_side([rows, next_, prev])
    w = border_terms(*partial, yp, ym, zp, zm)

    mate = lambda v: permuted(v, "gz", lambda s: s ^ 1)
    along_x = lambda v, step: permuted(v, "gy", lambda s: (s // 4) * 4 + (s + step) % 4)

    def row_sum(keep, send):
        chip = (keep + mate(send)).astype(BF16)
        return four_sum(chip, along_x(chip, 2), along_x(chip, 1), along_x(chip, 3)).astype(BF16)

    near = row_sum(*contract_near(w, right))
    far = row_sum(*contract_far(w, [far_low, far_high]))
    row = jnp.concatenate([near, far], 1)
    across = permuted(row, "gy", lambda s: s ^ 4)
    side = permuted(row, "gz", lambda s: s ^ 2)
    both = permuted(row, ("gz", "gy"), lambda s: s ^ 20)
    plane = four_sum(row, across, side, both)
    scale = 1.0 / math.sqrt(EXT_X * EXT_Y * EXT_Z)
    return finish(directions, plane, mate(plane), scale)


def solution(mesh):
    in_specs = (P("vec", None, "gz", "gy", None), P(None, None, None, "gz", "gy", None), P(), P())
    out_specs = P(None, None, "vec", None)
    return jax.shard_map(body, mesh=mesh, in_specs=in_specs, out_specs=out_specs, check_vma=False)
```

```python
import functools
import math

import jax
import jax.numpy as jnp
from jax import lax
from jax.experimental import pallas as pl
from jax.experimental.pallas import tpu as pltpu
from jax.sharding import PartitionSpec as P

F32 = jnp.float32
BF16 = jnp.bfloat16
VMEM = pl.BlockSpec(memory_space=pltpu.VMEM)
SMEM = pl.BlockSpec(memory_space=pltpu.SMEM)
ANY = pl.BlockSpec(memory_space=pl.ANY)
HBM = pl.BlockSpec(memory_space=pltpu.HBM)

NV = 64
COL = 3
DZ = 8
HY = 2
LANES = 128
HALF = 64
NZY = DZ * HY
EXT_X, EXT_Y, EXT_Z = 64, 16, 32
NK = COL * NZY
KDIM = NK * LANES


def params(limit):
    return pltpu.CompilerParams(vmem_limit_bytes=limit * 1024 * 1024)


def shape(dims, dtype):
    return jax.ShapeDtypeStruct(dims, dtype)


def fetch(sources, targets, sem):
    copies = [
        pltpu.make_async_copy(source, target, sem.at[i])
        for i, (source, target) in enumerate(zip(sources, targets))
    ]
    for copy in copies:
        copy.start()
    return copies


def prepare_kernel(rows, lrows, y0_ref, y1_ref, z0_ref, z1_ref, wide, lwide):
    wide[...] = rows[...].astype(F32)
    lwide[0:432, :] = lrows[...].astype(F32)
    lwide[432:576, :] = jnp.zeros((144, LANES), F32)
    for k in range(NK):
        tile = wide[pl.ds(k, NV, stride=NK), :].astype(BF16)
        c, z, y = k // NZY, (k % NZY) // HY, k % HY
        if y == 0:
            y0_ref[c * DZ + z] = tile
        else:
            y1_ref[c * DZ + z] = tile
        if z == 0:
            z0_ref[c * HY + y] = tile
        if z == DZ - 1:
            z1_ref[c * HY + y] = tile
    rim = lwide[pl.ds(9 * NZY + 1, 72, stride=HY), :]
    rim = jnp.concatenate([rim, jnp.zeros((56, LANES), F32)], 0).astype(BF16)
    y1_ref[24] = rim[0:64]
    y1_ref[25] = rim[64:128]
    low = lwide[pl.ds(18 * NZY + 14, 16, stride=NZY), :]
    high = lwide[pl.ds(18 * NZY + 15, 16, stride=NZY), :]
    rest = jnp.zeros((32, LANES), F32)
    z1_ref[6] = jnp.concatenate([low, high, rest], 0).astype(BF16)


def prepare(rows, link_rows):
    return pl.pallas_call(
        prepare_kernel,
        out_shape=(
            shape((24, NV, LANES), BF16),
            shape((26, NV, LANES), BF16),
            shape((6, NV, LANES), BF16),
            shape((7, NV, LANES), BF16),
        ),
        in_specs=[VMEM] * 2,
        out_specs=(VMEM,) * 4,
        scratch_shapes=[
            pltpu.VMEM((NV * NK, LANES), F32),
            pltpu.VMEM((576, LANES), F32),
        ],
        compiler_params=params(6),
        cost_estimate=pl.CostEstimate(flops=2000000000, bytes_accessed=3000000, transcendentals=0),
        name="prepare",
    )(rows, link_rows)


def line_coefficients(rows, first):
    half = rows * 0.5
    swapped = pltpu.roll(half, HALF, 1)
    return jnp.where(first, half, swapped), jnp.where(first, swapped, half)


def lane_masks():
    lane = lax.broadcasted_iota(jnp.int32, (1, LANES), 1)
    return lane, lane < HALF, jnp.where(lane < HALF, -1.0, 1.0).astype(F32)


def derivative(mu, neighbour, tables, zy, store):
    upr, upi, dnr, dni = tables
    out = [None] * 3
    for c in range(COL):
        here, swap = neighbour(c, 1)
        for r in range(3):
            at = mu * 9 + r * 3 + c
            term = here * upr[zy, at:at + 1, :] + swap * upi[zy, at:at + 1, :]
            out[r] = term if out[r] is None else out[r] + term
    for c in range(COL):
        here, swap = neighbour(c, -1)
        for r in range(3):
            at = mu * 9 + c * 3 + r
            term = here * dnr[zy, at:at + 1, :] - swap * dni[zy, at:at + 1, :]
            out[r] = out[r] - term
    for r in range(3):
        store(r, out[r].astype(BF16))


def local_kernel(
    momentum_ref, v_ref, l_ref, w_ref, ext, exts, upr, upi, dnr, dni,
    wide, lwide, real, imag, cos_ref, sin_ref,
):
    lane, first, sign = lane_masks()
    at = lax.broadcasted_iota(jnp.int32, (NZY, LANES), 0)
    x = lax.broadcasted_iota(jnp.int32, (NZY, LANES), 1) & (HALF - 1)
    y = lax.axis_index("gy").astype(jnp.int32) * HY + (at & (HY - 1))
    z = lax.axis_index("gz").astype(jnp.int32) * DZ + (at >> 1)
    frac_x = ((momentum_ref[0] * x) & (EXT_X - 1)).astype(F32) / EXT_X
    frac_y = ((momentum_ref[1] * y) & (EXT_Y - 1)).astype(F32) / EXT_Y
    frac_z = ((momentum_ref[2] * z) & (EXT_Z - 1)).astype(F32) / EXT_Z
    angle = 2.0 * math.pi * (frac_z + frac_y + frac_x)
    cos_ref[...] = jnp.cos(angle)
    sin_ref[...] = -sign * jnp.sin(angle)

    wide[...] = v_ref[...].astype(F32)
    for c in range(COL):
        for z in range(DZ):
            for y in range(HY):
                tile = wide[pl.ds((c * DZ + z) * HY + y, NV, stride=NK), :]
                ext[c, z + 1, y + 1] = tile
                exts[c, z + 1, y + 1] = pltpu.roll(tile, HALF, 1)

    lwide[...] = l_ref[...].astype(F32)
    re, im = line_coefficients(lwide[...], first)
    real[...] = re
    imag[...] = im
    for zy in range(NZY):
        z, y = zy // HY, zy % HY
        pick = pl.ds(zy, 27, stride=NZY)
        upr[zy, 0:27, :] = real[pick, :]
        upi[zy, 0:27, :] = imag[pick, :] * sign
        pick = pl.ds(zy, 9, stride=NZY)
        dnr[zy, 0:9, :] = pltpu.roll(real[pick, :], 1, 1)
        dni[zy, 0:9, :] = pltpu.roll(imag[pick, :], 1, 1) * sign
        if y:
            pick = pl.ds(9 * NZY + zy - 1, 9, stride=NZY)
            dnr[zy, 9:18, :] = real[pick, :]
            dni[zy, 9:18, :] = imag[pick, :] * sign
        if z:
            pick = pl.ds(18 * NZY + zy - HY, 9, stride=NZY)
            dnr[zy, 18:27, :] = real[pick, :]
            dni[zy, 18:27, :] = imag[pick, :] * sign

    wrap_up = (lane == HALF - 1) | (lane == LANES - 1)
    wrap_down = (lane == 0) | (lane == HALF)

    def site(zy, carry):
        z = lax.div(zy, HY) + 1
        y = lax.rem(zy, HY) + 1

        def neighbour(c, step):
            here, swap = ext[c, z, y], exts[c, z, y]
            a = pltpu.roll(here, (-step) % LANES, 1)
            b = pltpu.roll(swap, (-step) % LANES, 1)
            wrap = wrap_up if step == 1 else wrap_down
            return jnp.where(wrap, b, a), jnp.where(wrap, a, b)

        def store(r, value):
            column = pl.multiple_of((r * NZY + zy) * LANES, LANES)
            w_ref[0, :, pl.ds(column, LANES)] = value

        derivative(0, neighbour, (upr, upi, dnr, dni), zy, store)
        cosine = cos_ref[pl.ds(zy, 1), :]
        sine = sin_ref[pl.ds(zy, 1), :]
        for c in range(COL):
            column = pl.multiple_of((c * NZY + zy) * LANES, LANES)
            phased = ext[c, z, y] * cosine + exts[c, z, y] * sine
            w_ref[1, :, pl.ds(column, LANES)] = phased.astype(BF16)
        return carry

    lax.fori_loop(0, NZY, site, 0)


EXTENDED = (COL, DZ + 2, HY + 2, NV, LANES)
TABLE = (NZY, 32, LANES)


def local_terms(momentum, rows, link_rows):
    line = pltpu.VMEM((27 * NZY, LANES), F32)
    return pl.pallas_call(
        local_kernel,
        out_shape=(shape((4, NV, KDIM), BF16),)
        + (shape(EXTENDED, F32),) * 2
        + (shape(TABLE, F32),) * 4,
        in_specs=[SMEM] + [VMEM] * 2,
        out_specs=(VMEM,) * 7,
        scratch_shapes=[
            pltpu.VMEM((NV * NK, LANES), F32),
            line,
            line,
            line,
            pltpu.VMEM((NZY, LANES), F32),
            pltpu.VMEM((NZY, LANES), F32),
        ],
        compiler_params=params(8),
        cost_estimate=pl.CostEstimate(flops=6000000000, bytes_accessed=6000000, transcendentals=0),
        name="local_terms",
    )(momentum, rows, link_rows)


def border_kernel(
    local_ref, e_ref, s_ref, upr, upi, r_ref, i_ref, yp_ref, ym_ref, zp_ref, zm_ref,
    w_ref, ext, exts, dnr, dni, lwide, real, imag,
):
    lane, first, sign = lane_masks()

    def put(c, z, y, tile):
        tile = tile.astype(F32)
        ext[c, z, y] = tile
        exts[c, z, y] = pltpu.roll(tile, HALF, 1)

    for c in range(COL):
        for z in range(DZ):
            put(c, z + 1, HY + 1, yp_ref[c * DZ + z])
            put(c, z + 1, 0, ym_ref[c * DZ + z])
        for y in range(HY):
            put(c, DZ + 1, y + 1, zp_ref[c * HY + y])
            put(c, 0, y + 1, zm_ref[c * HY + y])

    lwide[0:128, :] = jnp.concatenate([ym_ref[24], ym_ref[25]], 0).astype(F32)
    lwide[128:192, :] = zm_ref[6].astype(F32)
    re, im = line_coefficients(lwide[...], first)
    real[...] = re
    imag[...] = im * sign
    for z in range(DZ):
        pick = pl.ds(z, 9, stride=DZ)
        dnr[z * HY, 9:18, :] = real[pick, :]
        dni[z * HY, 9:18, :] = imag[pick, :]
    for y in range(HY):
        pick = pl.ds(128 + 16 * y, 9)
        dnr[y, 18:27, :] = real[pick, :]
        dni[y, 18:27, :] = imag[pick, :]

    def site(zy, carry):
        z = lax.div(zy, HY) + 1
        y = lax.rem(zy, HY) + 1
        for mu in (1, 2):

            def neighbour(c, step):
                at = (c, z, y + step) if mu == 1 else (c, z + step, y)
                return ext[at], exts[at]

            def store(r, value):
                column = pl.multiple_of((r * NZY + zy) * LANES, LANES)
                w_ref[mu + 1, :, pl.ds(column, LANES)] = value

            derivative(mu, neighbour, (upr, upi, dnr, dni), zy, store)
        return carry

    lax.fori_loop(0, NZY, site, 0)


def border_terms(w, ext, exts, upr, upi, dnr, dni, yp, ym, zp, zm):
    line = pltpu.VMEM((192, LANES), F32)
    return pl.pallas_call(
        border_kernel,
        out_shape=(shape((4, NV, KDIM), BF16),)
        + (shape(EXTENDED, F32),) * 2
        + (shape(TABLE, F32),) * 2,
        in_specs=[VMEM] * 11,
        out_specs=(VMEM,) * 5,
        input_output_aliases={0: 0, 1: 1, 2: 2, 5: 3, 6: 4},
        scratch_shapes=[line, line, line],
        compiler_params=params(4),
        cost_estimate=pl.CostEstimate(flops=6000000000, bytes_accessed=6000000, transcendentals=0),
        name="border_terms",
    )(w, ext, exts, upr, upi, dnr, dni, yp, ym, zp, zm)[0]


def fill_right(counts, blocks, wide, right):
    total = sum(counts)
    lane, first, sign = lane_masks()
    start = 0
    for block, count in zip(blocks, counts):
        wide[0:count * NK, :] = block[...].astype(F32)
        for k in range(NK):
            tile = wide[pl.ds(k, count, stride=NK), :]
            swap = pltpu.roll(tile, HALF, 1) * sign
            right[start:start + count, k * LANES:(k + 1) * LANES] = tile.astype(BF16)
            right[total + start:total + start + count, k * LANES:(k + 1) * LANES] = swap.astype(BF16)
        start += count


def dot_halves(w_ref, right, keep_ref, send_ref, product):
    left = w_ref[...].reshape(4 * NV, KDIM)
    dots = lax.dot_general(left, right[...], (((1,), (1,)), ((), ())), preferred_element_type=F32)
    product[...] = dots.reshape(2, 2 * NV, dots.shape[1])
    mine = lax.axis_index("gz").astype(jnp.int32) & 1
    keep_ref[...] = product[mine]
    send_ref[...] = product[1 - mine]


def right_kernel(counts, *refs):
    n = len(counts)
    fill_right(counts, refs[:n], refs[n + 1], refs[n])


def right_side(blocks):
    counts = tuple(b.shape[0] // NK for b in blocks)
    return pl.pallas_call(
        functools.partial(right_kernel, counts),
        out_shape=shape((2 * sum(counts), KDIM), BF16),
        in_specs=[VMEM] * len(blocks),
        out_specs=VMEM,
        scratch_shapes=[pltpu.VMEM((max(counts) * NK, LANES), F32)],
        compiler_params=params(4),
        cost_estimate=pl.CostEstimate(flops=2000000000, bytes_accessed=4000000, transcendentals=0),
        name="right_side",
    )(*blocks)


def near_kernel(w_ref, right_ref, keep_ref, send_ref, product):
    dot_halves(w_ref, right_ref, keep_ref, send_ref, product)


def far_kernel(counts, w_ref, *refs):
    n = len(counts)
    keep_ref, send_ref, wide, right, product = refs[n:]
    fill_right(counts, refs[:n], wide, right)
    dot_halves(w_ref, right, keep_ref, send_ref, product)


def contract_near(w, right):
    columns = right.shape[0]
    out = shape((2 * NV, columns), F32)
    return pl.pallas_call(
        near_kernel,
        out_shape=(out, out),
        in_specs=[VMEM] * 2,
        out_specs=(VMEM, VMEM),
        scratch_shapes=[pltpu.VMEM((2, 2 * NV, columns), F32)],
        compiler_params=params(4),
        cost_estimate=pl.CostEstimate(
            flops=2 * 256 * columns * KDIM, bytes_accessed=4000000, transcendentals=0
        ),
        name="contract_near",
    )(w, right)


def contract_far(w, blocks):
    counts = tuple(b.shape[0] // NK for b in blocks)
    columns = 2 * sum(counts)
    out = shape((2 * NV, columns), F32)
    return pl.pallas_call(
        functools.partial(far_kernel, counts),
        out_shape=(out, out),
        in_specs=[VMEM] * (1 + len(blocks)),
        out_specs=(VMEM, VMEM),
        scratch_shapes=[
            pltpu.VMEM((max(counts) * NK, LANES), F32),
            pltpu.VMEM((columns, KDIM), BF16),
            pltpu.VMEM((2, 2 * NV, columns), F32),
        ],
        compiler_params=params(5),
        cost_estimate=pl.CostEstimate(
            flops=2 * 256 * columns * KDIM, bytes_accessed=4000000, transcendentals=0
        ),
        name="contract_far",
    )(w, *blocks)


def finish_kernel(scale, dirs_ref, mine_ref, other_ref, out_ref):
    shift = lax.axis_index("vec").astype(jnp.int32) * HALF
    core = lax.axis_index("gz").astype(jnp.int32) & 1
    slots = [
        sum(jnp.where(dirs_ref[o] == mu, o, 0) for o in range(3)).astype(jnp.int32)
        for mu in range(3)
    ]
    for ch, rows_ref in enumerate((mine_ref, other_ref)):
        rows = rows_ref[...]
        for part in range(2):
            near = rows[:, part * 192:(part + 1) * 192]
            far = rows[:, 384 + part * 64:384 + (part + 1) * 64]
            line = jnp.concatenate([near[:, 0:128], far, near[:, 128:192]], 1) * scale
            line = pltpu.roll(line, shift, 1)
            half = core if ch == 0 else 1 - core
            out_ref[jnp.where(half == 0, slots[0], slots[1]), part] = line[0:NV]
            out_ref[jnp.where(half == 0, 3, slots[2]), part] = line[NV:2 * NV]


def finish(directions, mine, other, scale):
    return pl.pallas_call(
        functools.partial(finish_kernel, scale),
        out_shape=shape((4, 2, NV, 256), F32),
        in_specs=[SMEM] + [VMEM] * 2,
        out_specs=VMEM,
        compiler_params=params(16),
        cost_estimate=pl.CostEstimate(flops=200000, bytes_accessed=1000000, transcendentals=0),
        name="finish",
    )(directions, mine, other)


def permuted(value, axis, target):
    size = lax.axis_size(axis)
    return lax.ppermute(value, axis, [(source, target(source)) for source in range(size)])


def four_sum(own, axis_opposite, axis_side, axis_other):
    wide = [t.astype(F32) for t in (own, axis_opposite, axis_side, axis_other)]
    return (wide[0] + wide[1]) + (wide[2] + wide[3])


def body(vectors, links, momentum, directions):
    rows = vectors.reshape(NV * NK, LANES)
    link_rows = links.reshape(27 * NZY, LANES)
    mid = NV * NK // 2
    prev = permuted(rows, "vec", lambda s: (s + 1) % 4)
    next_ = permuted(rows, "vec", lambda s: (s - 1) % 4)

    y0, y1, z0, z1 = prepare(rows, link_rows)
    yp = permuted(y0, "gy", lambda s: (s - 1) % 8)
    ym = permuted(y1, "gy", lambda s: (s + 1) % 8)
    zp = permuted(z0, "gz", lambda s: (s - 1) % 4)
    z1, zp = lax.optimization_barrier((z1, zp))
    zm = permuted(z1, "gz", lambda s: (s + 1) % 4)
    partial = local_terms(momentum, rows, link_rows)

    far_low = permuted(prev[:mid], "vec", lambda s: (s + 1) % 4)
    far_high = permuted(next_[mid:], "vec", lambda s: (s - 1) % 4)

    right = right_side([rows, next_, prev])
    yp, right = lax.optimization_barrier((yp, right))
    w = border_terms(*partial, yp, ym, zp, zm)

    mate = lambda v: permuted(v, "gz", lambda s: s ^ 1)
    along_x = lambda v, step: permuted(v, "gy", lambda s: (s // 4) * 4 + (s + step) % 4)

    def chip_sum(keep, send):
        return (keep + mate(send)).astype(BF16)

    near = chip_sum(*contract_near(w, right))
    far = chip_sum(*contract_far(w, [far_low, far_high]))
    chip = jnp.concatenate([near, far], 1)
    row = four_sum(chip, along_x(chip, 2), along_x(chip, 1), along_x(chip, 3)).astype(BF16)
    across = permuted(row, "gy", lambda s: s ^ 4)
    side = permuted(row, "gz", lambda s: s ^ 2)
    both = permuted(row, ("gz", "gy"), lambda s: s ^ 20)
    plane = four_sum(row, across, side, both)
    scale = 1.0 / math.sqrt(EXT_X * EXT_Y * EXT_Z)
    return finish(directions, plane, mate(plane), scale)


def solution(mesh):
    in_specs = (P("vec", None, "gz", "gy", None), P(None, None, None, "gz", "gy", None), P(), P())
    out_specs = P(None, None, "vec", None)
    return jax.shard_map(body, mesh=mesh, in_specs=in_specs, out_specs=out_specs, check_vma=False)
```

```python
import functools
import math

import jax
import jax.numpy as jnp
from jax import lax
from jax.experimental import pallas as pl
from jax.experimental.pallas import tpu as pltpu
from jax.sharding import PartitionSpec as P

F32 = jnp.float32
BF16 = jnp.bfloat16
VMEM = pl.BlockSpec(memory_space=pltpu.VMEM)
SMEM = pl.BlockSpec(memory_space=pltpu.SMEM)
ANY = pl.BlockSpec(memory_space=pl.ANY)
HBM = pl.BlockSpec(memory_space=pltpu.HBM)

NV = 64
COL = 3
DZ = 8
HY = 2
LANES = 128
HALF = 64
NZY = DZ * HY
EXT_X, EXT_Y, EXT_Z = 64, 16, 32
NK = COL * NZY
KDIM = NK * LANES


def params(limit):
    return pltpu.CompilerParams(vmem_limit_bytes=limit * 1024 * 1024)


def shape(dims, dtype):
    return jax.ShapeDtypeStruct(dims, dtype)


def fetch(sources, targets, sem):
    copies = [
        pltpu.make_async_copy(source, target, sem.at[i])
        for i, (source, target) in enumerate(zip(sources, targets))
    ]
    for copy in copies:
        copy.start()
    return copies


def prepare_kernel(rows, lrows, y0_ref, y1_ref, z0_ref, z1_ref, wide, lwide):
    wide[...] = rows[...].astype(F32)
    lwide[0:432, :] = lrows[...].astype(F32)
    lwide[432:576, :] = jnp.zeros((144, LANES), F32)
    for k in range(NK):
        tile = wide[pl.ds(k, NV, stride=NK), :].astype(BF16)
        c, z, y = k // NZY, (k % NZY) // HY, k % HY
        if y == 0:
            y0_ref[c * DZ + z] = tile
        else:
            y1_ref[c * DZ + z] = tile
        if z == 0:
            z0_ref[c * HY + y] = tile
        if z == DZ - 1:
            z1_ref[c * HY + y] = tile
    rim = lwide[pl.ds(9 * NZY + 1, 72, stride=HY), :]
    rim = jnp.concatenate([rim, jnp.zeros((56, LANES), F32)], 0).astype(BF16)
    y1_ref[24] = rim[0:64]
    y1_ref[25] = rim[64:128]
    low = lwide[pl.ds(18 * NZY + 14, 16, stride=NZY), :]
    high = lwide[pl.ds(18 * NZY + 15, 16, stride=NZY), :]
    rest = jnp.zeros((32, LANES), F32)
    z1_ref[6] = jnp.concatenate([low, high, rest], 0).astype(BF16)


def prepare(rows, link_rows):
    return pl.pallas_call(
        prepare_kernel,
        out_shape=(
            shape((24, NV, LANES), BF16),
            shape((26, NV, LANES), BF16),
            shape((6, NV, LANES), BF16),
            shape((7, NV, LANES), BF16),
        ),
        in_specs=[VMEM] * 2,
        out_specs=(VMEM,) * 4,
        scratch_shapes=[
            pltpu.VMEM((NV * NK, LANES), F32),
            pltpu.VMEM((576, LANES), F32),
        ],
        compiler_params=params(6),
        cost_estimate=pl.CostEstimate(flops=2000000000, bytes_accessed=3000000, transcendentals=0),
        name="prepare",
    )(rows, link_rows)


def line_coefficients(rows, first):
    half = rows * 0.5
    swapped = pltpu.roll(half, HALF, 1)
    return jnp.where(first, half, swapped), jnp.where(first, swapped, half)


def lane_masks():
    lane = lax.broadcasted_iota(jnp.int32, (1, LANES), 1)
    return lane, lane < HALF, jnp.where(lane < HALF, -1.0, 1.0).astype(F32)


def derivative(mu, neighbour, tables, zy, store):
    upr, upi, dnr, dni = tables
    out = [None] * 3
    for c in range(COL):
        here, swap = neighbour(c, 1)
        for r in range(3):
            at = mu * 9 + r * 3 + c
            term = here * upr[zy, at:at + 1, :] + swap * upi[zy, at:at + 1, :]
            out[r] = term if out[r] is None else out[r] + term
    for c in range(COL):
        here, swap = neighbour(c, -1)
        for r in range(3):
            at = mu * 9 + c * 3 + r
            term = here * dnr[zy, at:at + 1, :] - swap * dni[zy, at:at + 1, :]
            out[r] = out[r] - term
    for r in range(3):
        store(r, out[r].astype(BF16))


def local_kernel(
    momentum_ref, v_ref, l_ref, w_ref, ext, exts, upr, upi, dnr, dni,
    wide, lwide, real, imag, cos_ref, sin_ref,
):
    lane, first, sign = lane_masks()
    at = lax.broadcasted_iota(jnp.int32, (NZY, LANES), 0)
    x = lax.broadcasted_iota(jnp.int32, (NZY, LANES), 1) & (HALF - 1)
    y = lax.axis_index("gy").astype(jnp.int32) * HY + (at & (HY - 1))
    z = lax.axis_index("gz").astype(jnp.int32) * DZ + (at >> 1)
    frac_x = ((momentum_ref[0] * x) & (EXT_X - 1)).astype(F32) / EXT_X
    frac_y = ((momentum_ref[1] * y) & (EXT_Y - 1)).astype(F32) / EXT_Y
    frac_z = ((momentum_ref[2] * z) & (EXT_Z - 1)).astype(F32) / EXT_Z
    angle = 2.0 * math.pi * (frac_z + frac_y + frac_x)
    cos_ref[...] = jnp.cos(angle)
    sin_ref[...] = -sign * jnp.sin(angle)

    wide[...] = v_ref[...].astype(F32)
    for c in range(COL):
        for z in range(DZ):
            for y in range(HY):
                tile = wide[pl.ds((c * DZ + z) * HY + y, NV, stride=NK), :]
                ext[c, z + 1, y + 1] = tile
                exts[c, z + 1, y + 1] = pltpu.roll(tile, HALF, 1)

    lwide[...] = l_ref[...].astype(F32)
    re, im = line_coefficients(lwide[...], first)
    real[...] = re
    imag[...] = im
    for zy in range(NZY):
        z, y = zy // HY, zy % HY
        pick = pl.ds(zy, 27, stride=NZY)
        upr[zy, 0:27, :] = real[pick, :]
        upi[zy, 0:27, :] = imag[pick, :] * sign
        pick = pl.ds(zy, 9, stride=NZY)
        dnr[zy, 0:9, :] = pltpu.roll(real[pick, :], 1, 1)
        dni[zy, 0:9, :] = pltpu.roll(imag[pick, :], 1, 1) * sign
        if y:
            pick = pl.ds(9 * NZY + zy - 1, 9, stride=NZY)
            dnr[zy, 9:18, :] = real[pick, :]
            dni[zy, 9:18, :] = imag[pick, :] * sign
        if z:
            pick = pl.ds(18 * NZY + zy - HY, 9, stride=NZY)
            dnr[zy, 18:27, :] = real[pick, :]
            dni[zy, 18:27, :] = imag[pick, :] * sign

    wrap_up = (lane == HALF - 1) | (lane == LANES - 1)
    wrap_down = (lane == 0) | (lane == HALF)

    def site(zy, carry):
        z = lax.div(zy, HY) + 1
        y = lax.rem(zy, HY) + 1

        def neighbour(c, step):
            here, swap = ext[c, z, y], exts[c, z, y]
            a = pltpu.roll(here, (-step) % LANES, 1)
            b = pltpu.roll(swap, (-step) % LANES, 1)
            wrap = wrap_up if step == 1 else wrap_down
            return jnp.where(wrap, b, a), jnp.where(wrap, a, b)

        def store(r, value):
            column = pl.multiple_of((r * NZY + zy) * LANES, LANES)
            w_ref[0, :, pl.ds(column, LANES)] = value

        derivative(0, neighbour, (upr, upi, dnr, dni), zy, store)
        cosine = cos_ref[pl.ds(zy, 1), :]
        sine = sin_ref[pl.ds(zy, 1), :]
        for c in range(COL):
            column = pl.multiple_of((c * NZY + zy) * LANES, LANES)
            phased = ext[c, z, y] * cosine + exts[c, z, y] * sine
            w_ref[1, :, pl.ds(column, LANES)] = phased.astype(BF16)
        return carry

    lax.fori_loop(0, NZY, site, 0)


EXTENDED = (COL, DZ + 2, HY + 2, NV, LANES)
TABLE = (NZY, 32, LANES)


def local_terms(momentum, rows, link_rows):
    line = pltpu.VMEM((27 * NZY, LANES), F32)
    return pl.pallas_call(
        local_kernel,
        out_shape=(shape((4, NV, KDIM), BF16),)
        + (shape(EXTENDED, F32),) * 2
        + (shape(TABLE, F32),) * 4,
        in_specs=[SMEM] + [VMEM] * 2,
        out_specs=(VMEM,) * 7,
        scratch_shapes=[
            pltpu.VMEM((NV * NK, LANES), F32),
            line,
            line,
            line,
            pltpu.VMEM((NZY, LANES), F32),
            pltpu.VMEM((NZY, LANES), F32),
        ],
        compiler_params=params(8),
        cost_estimate=pl.CostEstimate(flops=6000000000, bytes_accessed=6000000, transcendentals=0),
        name="local_terms",
    )(momentum, rows, link_rows)


def border_kernel(
    mu, before_ref, e_ref, s_ref, upr, upi, r_ref, i_ref, ahead_ref, behind_ref,
    w_ref, ext, exts, dnr, dni, lwide, real, imag,
):
    lane, first, sign = lane_masks()

    def put(c, z, y, tile):
        tile = tile.astype(F32)
        ext[c, z, y] = tile
        exts[c, z, y] = pltpu.roll(tile, HALF, 1)

    for c in range(COL):
        if mu == 1:
            for z in range(DZ):
                put(c, z + 1, HY + 1, ahead_ref[c * DZ + z])
                put(c, z + 1, 0, behind_ref[c * DZ + z])
        else:
            for y in range(HY):
                put(c, DZ + 1, y + 1, ahead_ref[c * HY + y])
                put(c, 0, y + 1, behind_ref[c * HY + y])

    if mu == 1:
        lwide[...] = jnp.concatenate([behind_ref[24], behind_ref[25]], 0).astype(F32)
    else:
        lwide[0:64, :] = behind_ref[6].astype(F32)
        lwide[64:128, :] = jnp.zeros((64, LANES), F32)
    re, im = line_coefficients(lwide[...], first)
    real[...] = re
    imag[...] = im * sign
    if mu == 1:
        for z in range(DZ):
            pick = pl.ds(z, 9, stride=DZ)
            dnr[z * HY, 9:18, :] = real[pick, :]
            dni[z * HY, 9:18, :] = imag[pick, :]
    else:
        for y in range(HY):
            pick = pl.ds(16 * y, 9)
            dnr[y, 18:27, :] = real[pick, :]
            dni[y, 18:27, :] = imag[pick, :]

    def site(zy, carry):
        z = lax.div(zy, HY) + 1
        y = lax.rem(zy, HY) + 1

        def neighbour(c, step):
            at = (c, z, y + step) if mu == 1 else (c, z + step, y)
            return ext[at], exts[at]

        def store(r, value):
            column = pl.multiple_of((r * NZY + zy) * LANES, LANES)
            w_ref[mu + 1, :, pl.ds(column, LANES)] = value

        derivative(mu, neighbour, (upr, upi, dnr, dni), zy, store)
        return carry

    lax.fori_loop(0, NZY, site, 0)


def border_terms(mu, w, ext, exts, upr, upi, dnr, dni, ahead, behind):
    line = pltpu.VMEM((128, LANES), F32)
    w, ext, exts, dnr, dni = pl.pallas_call(
        functools.partial(border_kernel, mu),
        out_shape=(shape((4, NV, KDIM), BF16),)
        + (shape(EXTENDED, F32),) * 2
        + (shape(TABLE, F32),) * 2,
        in_specs=[VMEM] * 9,
        out_specs=(VMEM,) * 5,
        input_output_aliases={0: 0, 1: 1, 2: 2, 5: 3, 6: 4},
        scratch_shapes=[line, line, line],
        compiler_params=params(4),
        cost_estimate=pl.CostEstimate(flops=3000000000, bytes_accessed=3000000, transcendentals=0),
        name="border_y" if mu == 1 else "border_z",
    )(w, ext, exts, upr, upi, dnr, dni, ahead, behind)
    return w, ext, exts, upr, upi, dnr, dni


def fill_right(counts, blocks, wide, right):
    total = sum(counts)
    lane, first, sign = lane_masks()
    start = 0
    for block, count in zip(blocks, counts):
        wide[0:count * NK, :] = block[...].astype(F32)
        for k in range(NK):
            tile = wide[pl.ds(k, count, stride=NK), :]
            swap = pltpu.roll(tile, HALF, 1) * sign
            right[start:start + count, k * LANES:(k + 1) * LANES] = tile.astype(BF16)
            right[total + start:total + start + count, k * LANES:(k + 1) * LANES] = swap.astype(BF16)
        start += count


def dot_halves(w_ref, right, keep_ref, send_ref, product):
    left = w_ref[...].reshape(4 * NV, KDIM)
    dots = lax.dot_general(left, right[...], (((1,), (1,)), ((), ())), preferred_element_type=F32)
    product[...] = dots.reshape(2, 2 * NV, dots.shape[1])
    mine = lax.axis_index("gz").astype(jnp.int32) & 1
    keep_ref[...] = product[mine]
    send_ref[...] = product[1 - mine]


def right_kernel(counts, *refs):
    n = len(counts)
    fill_right(counts, refs[:n], refs[n + 1], refs[n])


def right_side(blocks):
    counts = tuple(b.shape[0] // NK for b in blocks)
    return pl.pallas_call(
        functools.partial(right_kernel, counts),
        out_shape=shape((2 * sum(counts), KDIM), BF16),
        in_specs=[VMEM] * len(blocks),
        out_specs=VMEM,
        scratch_shapes=[pltpu.VMEM((max(counts) * NK, LANES), F32)],
        compiler_params=params(4),
        cost_estimate=pl.CostEstimate(flops=2000000000, bytes_accessed=4000000, transcendentals=0),
        name="right_side",
    )(*blocks)


def near_kernel(w_ref, right_ref, keep_ref, send_ref, product):
    dot_halves(w_ref, right_ref, keep_ref, send_ref, product)


def far_kernel(counts, w_ref, *refs):
    n = len(counts)
    keep_ref, send_ref, wide, right, product = refs[n:]
    fill_right(counts, refs[:n], wide, right)
    dot_halves(w_ref, right, keep_ref, send_ref, product)


def contract_near(w, right):
    columns = right.shape[0]
    out = shape((2 * NV, columns), F32)
    return pl.pallas_call(
        near_kernel,
        out_shape=(out, out),
        in_specs=[VMEM] * 2,
        out_specs=(VMEM, VMEM),
        scratch_shapes=[pltpu.VMEM((2, 2 * NV, columns), F32)],
        compiler_params=params(4),
        cost_estimate=pl.CostEstimate(
            flops=2 * 256 * columns * KDIM, bytes_accessed=4000000, transcendentals=0
        ),
        name="contract_near",
    )(w, right)


def contract_far(w, blocks):
    counts = tuple(b.shape[0] // NK for b in blocks)
    columns = 2 * sum(counts)
    out = shape((2 * NV, columns), F32)
    return pl.pallas_call(
        functools.partial(far_kernel, counts),
        out_shape=(out, out),
        in_specs=[VMEM] * (1 + len(blocks)),
        out_specs=(VMEM, VMEM),
        scratch_shapes=[
            pltpu.VMEM((max(counts) * NK, LANES), F32),
            pltpu.VMEM((columns, KDIM), BF16),
            pltpu.VMEM((2, 2 * NV, columns), F32),
        ],
        compiler_params=params(5),
        cost_estimate=pl.CostEstimate(
            flops=2 * 256 * columns * KDIM, bytes_accessed=4000000, transcendentals=0
        ),
        name="contract_far",
    )(w, *blocks)


def finish_kernel(scale, other, dirs_ref, rows_ref, *refs):
    out_ref, lines, sem = refs[-3:]
    shift = lax.axis_index("vec").astype(jnp.int32) * HALF
    half = (lax.axis_index("gz").astype(jnp.int32) & 1) ^ other
    slots = [
        sum(jnp.where(dirs_ref[o] == mu, o, 0) for o in range(3)).astype(jnp.int32)
        for mu in range(3)
    ]
    places = [jnp.where(half == 0, slots[0], slots[1]), jnp.where(half == 0, 3, slots[2])]
    rows = rows_ref[...]
    copies = []
    for part in range(2):
        near = rows[:, part * 192:(part + 1) * 192]
        far = rows[:, 384 + part * 64:384 + (part + 1) * 64]
        line = jnp.concatenate([near[:, 0:128], far, near[:, 128:192]], 1) * scale
        line = pltpu.roll(line, shift, 1)
        for which in range(2):
            lines[which, part] = line[which * NV:(which + 1) * NV]
            copy = pltpu.make_async_copy(
                lines.at[which, part], out_ref.at[places[which], part], sem.at[which, part]
            )
            copy.start()
            copies.append(copy)
    for copy in copies:
        copy.wait()


def finish(directions, rows, scale, so_far=None):
    other = so_far is not None
    return pl.pallas_call(
        functools.partial(finish_kernel, scale, int(other)),
        out_shape=shape((4, 2, NV, 256), F32),
        in_specs=[SMEM, VMEM] + [HBM] * other,
        out_specs=HBM,
        input_output_aliases={2: 0} if other else {},
        scratch_shapes=[pltpu.VMEM((2, 2, NV, 256), F32), pltpu.SemaphoreType.DMA((2, 2))],
        compiler_params=params(4),
        cost_estimate=pl.CostEstimate(flops=200000, bytes_accessed=1000000, transcendentals=0),
        name="finish_other" if other else "finish_mine",
    )(directions, rows, *([so_far] if other else []))


def permuted(value, axis, target):
    size = lax.axis_size(axis)
    return lax.ppermute(value, axis, [(source, target(source)) for source in range(size)])


def four_sum(own, opposite, side, other):
    pair = side.astype(F32) + other.astype(F32)
    return pair + (own.astype(F32) + opposite.astype(F32))


def body(vectors, links, momentum, directions):
    rows = vectors.reshape(NV * NK, LANES)
    link_rows = links.reshape(27 * NZY, LANES)
    mid = NV * NK // 2
    prev = permuted(rows, "vec", lambda s: (s + 1) % 4)
    next_ = permuted(rows, "vec", lambda s: (s - 1) % 4)

    y0, y1, z0, z1 = prepare(rows, link_rows)
    yp = permuted(y0, "gy", lambda s: (s - 1) % 8)
    ym = permuted(y1, "gy", lambda s: (s + 1) % 8)
    zp = permuted(z0, "gz", lambda s: (s - 1) % 4)
    z1, zp = lax.optimization_barrier((z1, zp))
    zm = permuted(z1, "gz", lambda s: (s + 1) % 4)
    partial = local_terms(momentum, rows, link_rows)

    far_low = permuted(prev[:mid], "vec", lambda s: (s + 1) % 4)
    far_high = permuted(next_[mid:], "vec", lambda s: (s - 1) % 4)

    right = right_side([rows, next_, prev])
    zm, right = lax.optimization_barrier((zm, right))
    partial = border_terms(2, *partial, zp, zm)
    w = border_terms(1, *partial, yp, ym)[0]

    mate = lambda v: permuted(v, "gz", lambda s: s ^ 1)
    along_x = lambda v, step: permuted(v, "gy", lambda s: (s // 4) * 4 + (s + step) % 4)

    def chip_sum(keep, send):
        return (keep + mate(send)).astype(BF16)

    near = chip_sum(*contract_near(w, right))
    far = chip_sum(*contract_far(w, [far_low, far_high]))
    chip = jnp.concatenate([near, far], 1)
    ahead, behind = along_x(chip, 1), along_x(chip, 3)
    row = four_sum(chip, along_x(chip, 2), ahead, behind).astype(BF16)
    side = permuted(row, "gz", lambda s: s ^ 2)
    both = permuted(row, ("gz", "gy"), lambda s: s ^ 20)
    across = permuted(row, "gy", lambda s: s ^ 4)
    plane = four_sum(row, across, side, both)
    scale = 1.0 / math.sqrt(EXT_X * EXT_Y * EXT_Z)
    mine = finish(directions, plane, scale)
    return finish(directions, mate(plane), scale, mine)


def solution(mesh):
    in_specs = (P("vec", None, "gz", "gy", None), P(None, None, None, "gz", "gy", None), P(), P())
    out_specs = P(None, None, "vec", None)
    return jax.shard_map(body, mesh=mesh, in_specs=in_specs, out_specs=out_specs, check_vma=False)
```

```python
import functools
import math

import jax
import jax.numpy as jnp
from jax import lax
from jax.experimental import pallas as pl
from jax.experimental.pallas import tpu as pltpu
from jax.sharding import PartitionSpec as P

F32 = jnp.float32
BF16 = jnp.bfloat16
VMEM = pl.BlockSpec(memory_space=pltpu.VMEM)
SMEM = pl.BlockSpec(memory_space=pltpu.SMEM)
ANY = pl.BlockSpec(memory_space=pl.ANY)
HBM = pl.BlockSpec(memory_space=pltpu.HBM)

NV = 64
COL = 3
DZ = 8
HY = 2
LANES = 128
HALF = 64
NZY = DZ * HY
EXT_X, EXT_Y, EXT_Z = 64, 16, 32
NK = COL * NZY
KDIM = NK * LANES


def params(limit):
    return pltpu.CompilerParams(vmem_limit_bytes=limit * 1024 * 1024)


def shape(dims, dtype):
    return jax.ShapeDtypeStruct(dims, dtype)


def fetch(sources, targets, sem):
    copies = [
        pltpu.make_async_copy(source, target, sem.at[i])
        for i, (source, target) in enumerate(zip(sources, targets))
    ]
    for copy in copies:
        copy.start()
    return copies


def prepare_kernel(rows, lrows, y0_ref, y1_ref, z0_ref, z1_ref, wide, lwide):
    wide[...] = rows[...].astype(F32)
    lwide[0:432, :] = lrows[...].astype(F32)
    lwide[432:576, :] = jnp.zeros((144, LANES), F32)
    for k in range(NK):
        tile = wide[pl.ds(k, NV, stride=NK), :].astype(BF16)
        c, z, y = k // NZY, (k % NZY) // HY, k % HY
        if y == 0:
            y0_ref[c * DZ + z] = tile
        else:
            y1_ref[c * DZ + z] = tile
        if z == 0:
            z0_ref[c * HY + y] = tile
        if z == DZ - 1:
            z1_ref[c * HY + y] = tile
    rim = lwide[pl.ds(9 * NZY + 1, 72, stride=HY), :]
    rim = jnp.concatenate([rim, jnp.zeros((56, LANES), F32)], 0).astype(BF16)
    y1_ref[24] = rim[0:64]
    y1_ref[25] = rim[64:128]
    low = lwide[pl.ds(18 * NZY + 14, 16, stride=NZY), :]
    high = lwide[pl.ds(18 * NZY + 15, 16, stride=NZY), :]
    rest = jnp.zeros((32, LANES), F32)
    z1_ref[6] = jnp.concatenate([low, high, rest], 0).astype(BF16)


def prepare(rows, link_rows):
    return pl.pallas_call(
        prepare_kernel,
        out_shape=(
            shape((24, NV, LANES), BF16),
            shape((26, NV, LANES), BF16),
            shape((6, NV, LANES), BF16),
            shape((7, NV, LANES), BF16),
        ),
        in_specs=[VMEM] * 2,
        out_specs=(VMEM,) * 4,
        scratch_shapes=[
            pltpu.VMEM((NV * NK, LANES), F32),
            pltpu.VMEM((576, LANES), F32),
        ],
        compiler_params=params(6),
        cost_estimate=pl.CostEstimate(flops=2000000000, bytes_accessed=3000000, transcendentals=0),
        name="prepare",
    )(rows, link_rows)


def line_coefficients(rows, first):
    half = rows * 0.5
    swapped = pltpu.roll(half, HALF, 1)
    return jnp.where(first, half, swapped), jnp.where(first, swapped, half)


def lane_masks():
    lane = lax.broadcasted_iota(jnp.int32, (1, LANES), 1)
    return lane, lane < HALF, jnp.where(lane < HALF, -1.0, 1.0).astype(F32)


def derivative(mu, neighbour, tables, zy, store):
    upr, upi, dnr, dni = tables
    out = [None] * 3
    for c in range(COL):
        here, swap = neighbour(c, 1)
        for r in range(3):
            at = mu * 9 + r * 3 + c
            term = here * upr[zy, at:at + 1, :] + swap * upi[zy, at:at + 1, :]
            out[r] = term if out[r] is None else out[r] + term
    for c in range(COL):
        here, swap = neighbour(c, -1)
        for r in range(3):
            at = mu * 9 + c * 3 + r
            term = here * dnr[zy, at:at + 1, :] - swap * dni[zy, at:at + 1, :]
            out[r] = out[r] - term
    for r in range(3):
        store(r, out[r].astype(BF16))


def local_kernel(
    momentum_ref, v_ref, l_ref, w_ref, ext, exts, upr, upi, dnr, dni,
    wide, lwide, real, imag, cos_ref, sin_ref,
):
    lane, first, sign = lane_masks()
    at = lax.broadcasted_iota(jnp.int32, (NZY, LANES), 0)
    x = lax.broadcasted_iota(jnp.int32, (NZY, LANES), 1) & (HALF - 1)
    y = lax.axis_index("gy").astype(jnp.int32) * HY + (at & (HY - 1))
    z = lax.axis_index("gz").astype(jnp.int32) * DZ + (at >> 1)
    frac_x = ((momentum_ref[0] * x) & (EXT_X - 1)).astype(F32) / EXT_X
    frac_y = ((momentum_ref[1] * y) & (EXT_Y - 1)).astype(F32) / EXT_Y
    frac_z = ((momentum_ref[2] * z) & (EXT_Z - 1)).astype(F32) / EXT_Z
    angle = 2.0 * math.pi * (frac_z + frac_y + frac_x)
    cos_ref[...] = jnp.cos(angle)
    sin_ref[...] = -sign * jnp.sin(angle)

    wide[...] = v_ref[...].astype(F32)
    for c in range(COL):
        for z in range(DZ):
            for y in range(HY):
                tile = wide[pl.ds((c * DZ + z) * HY + y, NV, stride=NK), :]
                ext[c, z + 1, y + 1] = tile
                exts[c, z + 1, y + 1] = pltpu.roll(tile, HALF, 1)

    lwide[...] = l_ref[...].astype(F32)
    re, im = line_coefficients(lwide[...], first)
    real[...] = re
    imag[...] = im
    for zy in range(NZY):
        z, y = zy // HY, zy % HY
        pick = pl.ds(zy, 27, stride=NZY)
        upr[zy, 0:27, :] = real[pick, :]
        upi[zy, 0:27, :] = imag[pick, :] * sign
        pick = pl.ds(zy, 9, stride=NZY)
        dnr[zy, 0:9, :] = pltpu.roll(real[pick, :], 1, 1)
        dni[zy, 0:9, :] = pltpu.roll(imag[pick, :], 1, 1) * sign
        if y:
            pick = pl.ds(9 * NZY + zy - 1, 9, stride=NZY)
            dnr[zy, 9:18, :] = real[pick, :]
            dni[zy, 9:18, :] = imag[pick, :] * sign
        if z:
            pick = pl.ds(18 * NZY + zy - HY, 9, stride=NZY)
            dnr[zy, 18:27, :] = real[pick, :]
            dni[zy, 18:27, :] = imag[pick, :] * sign

    wrap_up = (lane == HALF - 1) | (lane == LANES - 1)
    wrap_down = (lane == 0) | (lane == HALF)

    def site(zy, carry):
        z = lax.div(zy, HY) + 1
        y = lax.rem(zy, HY) + 1

        def neighbour(c, step):
            here, swap = ext[c, z, y], exts[c, z, y]
            a = pltpu.roll(here, (-step) % LANES, 1)
            b = pltpu.roll(swap, (-step) % LANES, 1)
            wrap = wrap_up if step == 1 else wrap_down
            return jnp.where(wrap, b, a), jnp.where(wrap, a, b)

        def store(r, value):
            column = pl.multiple_of((r * NZY + zy) * LANES, LANES)
            w_ref[0, :, pl.ds(column, LANES)] = value

        derivative(0, neighbour, (upr, upi, dnr, dni), zy, store)
        cosine = cos_ref[pl.ds(zy, 1), :]
        sine = sin_ref[pl.ds(zy, 1), :]
        for c in range(COL):
            column = pl.multiple_of((c * NZY + zy) * LANES, LANES)
            phased = ext[c, z, y] * cosine + exts[c, z, y] * sine
            w_ref[1, :, pl.ds(column, LANES)] = phased.astype(BF16)
        return carry

    lax.fori_loop(0, NZY, site, 0)


EXTENDED = (COL, DZ + 2, HY + 2, NV, LANES)
TABLE = (NZY, 32, LANES)


def local_terms(momentum, rows, link_rows):
    line = pltpu.VMEM((27 * NZY, LANES), F32)
    return pl.pallas_call(
        local_kernel,
        out_shape=(shape((4, NV, KDIM), BF16),)
        + (shape(EXTENDED, F32),) * 2
        + (shape(TABLE, F32),) * 4,
        in_specs=[SMEM] + [VMEM] * 2,
        out_specs=(VMEM,) * 7,
        scratch_shapes=[
            pltpu.VMEM((NV * NK, LANES), F32),
            line,
            line,
            line,
            pltpu.VMEM((NZY, LANES), F32),
            pltpu.VMEM((NZY, LANES), F32),
        ],
        compiler_params=params(8),
        cost_estimate=pl.CostEstimate(flops=6000000000, bytes_accessed=6000000, transcendentals=0),
        name="local_terms",
    )(momentum, rows, link_rows)


def border_kernel(
    mu, before_ref, e_ref, s_ref, upr, upi, r_ref, i_ref, ahead_ref, behind_ref,
    w_ref, ext, exts, dnr, dni, lwide, real, imag,
):
    lane, first, sign = lane_masks()

    def put(c, z, y, tile):
        tile = tile.astype(F32)
        ext[c, z, y] = tile
        exts[c, z, y] = pltpu.roll(tile, HALF, 1)

    for c in range(COL):
        if mu == 1:
            for z in range(DZ):
                put(c, z + 1, HY + 1, ahead_ref[c * DZ + z])
                put(c, z + 1, 0, behind_ref[c * DZ + z])
        else:
            for y in range(HY):
                put(c, DZ + 1, y + 1, ahead_ref[c * HY + y])
                put(c, 0, y + 1, behind_ref[c * HY + y])

    if mu == 1:
        lwide[...] = jnp.concatenate([behind_ref[24], behind_ref[25]], 0).astype(F32)
    else:
        lwide[0:64, :] = behind_ref[6].astype(F32)
        lwide[64:128, :] = jnp.zeros((64, LANES), F32)
    re, im = line_coefficients(lwide[...], first)
    real[...] = re
    imag[...] = im * sign
    if mu == 1:
        for z in range(DZ):
            pick = pl.ds(z, 9, stride=DZ)
            dnr[z * HY, 9:18, :] = real[pick, :]
            dni[z * HY, 9:18, :] = imag[pick, :]
    else:
        for y in range(HY):
            pick = pl.ds(16 * y, 9)
            dnr[y, 18:27, :] = real[pick, :]
            dni[y, 18:27, :] = imag[pick, :]

    def site(zy, carry):
        z = lax.div(zy, HY) + 1
        y = lax.rem(zy, HY) + 1

        def neighbour(c, step):
            at = (c, z, y + step) if mu == 1 else (c, z + step, y)
            return ext[at], exts[at]

        def store(r, value):
            column = pl.multiple_of((r * NZY + zy) * LANES, LANES)
            w_ref[mu + 1, :, pl.ds(column, LANES)] = value

        derivative(mu, neighbour, (upr, upi, dnr, dni), zy, store)
        return carry

    lax.fori_loop(0, NZY, site, 0)


def border_terms(mu, w, ext, exts, upr, upi, dnr, dni, ahead, behind):
    line = pltpu.VMEM((128, LANES), F32)
    w, ext, exts, dnr, dni = pl.pallas_call(
        functools.partial(border_kernel, mu),
        out_shape=(shape((4, NV, KDIM), BF16),)
        + (shape(EXTENDED, F32),) * 2
        + (shape(TABLE, F32),) * 2,
        in_specs=[VMEM] * 9,
        out_specs=(VMEM,) * 5,
        input_output_aliases={0: 0, 1: 1, 2: 2, 5: 3, 6: 4},
        scratch_shapes=[line, line, line],
        compiler_params=params(4),
        cost_estimate=pl.CostEstimate(flops=3000000000, bytes_accessed=3000000, transcendentals=0),
        name="border_y" if mu == 1 else "border_z",
    )(w, ext, exts, upr, upi, dnr, dni, ahead, behind)
    return w, ext, exts, upr, upi, dnr, dni


def fill_right(counts, blocks, wide, right):
    total = sum(counts)
    lane, first, sign = lane_masks()
    start = 0
    for block, count in zip(blocks, counts):
        wide[0:count * NK, :] = block[...].astype(F32)
        for k in range(NK):
            tile = wide[pl.ds(k, count, stride=NK), :]
            swap = pltpu.roll(tile, HALF, 1) * sign
            right[start:start + count, k * LANES:(k + 1) * LANES] = tile.astype(BF16)
            right[total + start:total + start + count, k * LANES:(k + 1) * LANES] = swap.astype(BF16)
        start += count


def dot_halves(w_ref, right, keep_ref, send_ref, product):
    left = w_ref[...].reshape(4 * NV, KDIM)
    dots = lax.dot_general(left, right[...], (((1,), (1,)), ((), ())), preferred_element_type=F32)
    product[...] = dots.reshape(2, 2 * NV, dots.shape[1])
    mine = lax.axis_index("gz").astype(jnp.int32) & 1
    keep_ref[...] = product[mine]
    send_ref[...] = product[1 - mine]


def right_kernel(counts, *refs):
    n = len(counts)
    fill_right(counts, refs[:n], refs[n + 1], refs[n])


def right_side(blocks):
    counts = tuple(b.shape[0] // NK for b in blocks)
    return pl.pallas_call(
        functools.partial(right_kernel, counts),
        out_shape=shape((2 * sum(counts), KDIM), BF16),
        in_specs=[VMEM] * len(blocks),
        out_specs=VMEM,
        scratch_shapes=[pltpu.VMEM((max(counts) * NK, LANES), F32)],
        compiler_params=params(4),
        cost_estimate=pl.CostEstimate(flops=2000000000, bytes_accessed=4000000, transcendentals=0),
        name="right_side",
    )(*blocks)


def near_kernel(w_ref, right_ref, keep_ref, send_ref, product):
    dot_halves(w_ref, right_ref, keep_ref, send_ref, product)


def far_kernel(counts, w_ref, *refs):
    n = len(counts)
    keep_ref, send_ref, wide, right, product = refs[n:]
    fill_right(counts, refs[:n], wide, right)
    dot_halves(w_ref, right, keep_ref, send_ref, product)


def contract_near(w, right):
    columns = right.shape[0]
    out = shape((2 * NV, columns), F32)
    return pl.pallas_call(
        near_kernel,
        out_shape=(out, out),
        in_specs=[VMEM] * 2,
        out_specs=(VMEM, VMEM),
        scratch_shapes=[pltpu.VMEM((2, 2 * NV, columns), F32)],
        compiler_params=params(4),
        cost_estimate=pl.CostEstimate(
            flops=2 * 256 * columns * KDIM, bytes_accessed=4000000, transcendentals=0
        ),
        name="contract_near",
    )(w, right)


def contract_far(w, blocks):
    counts = tuple(b.shape[0] // NK for b in blocks)
    columns = 2 * sum(counts)
    out = shape((2 * NV, columns), F32)
    return pl.pallas_call(
        functools.partial(far_kernel, counts),
        out_shape=(out, out),
        in_specs=[VMEM] * (1 + len(blocks)),
        out_specs=(VMEM, VMEM),
        scratch_shapes=[
            pltpu.VMEM((max(counts) * NK, LANES), F32),
            pltpu.VMEM((columns, KDIM), BF16),
            pltpu.VMEM((2, 2 * NV, columns), F32),
        ],
        compiler_params=params(5),
        cost_estimate=pl.CostEstimate(
            flops=2 * 256 * columns * KDIM, bytes_accessed=4000000, transcendentals=0
        ),
        name="contract_far",
    )(w, *blocks)


def finish_kernel(scale, other, dirs_ref, rows_ref, *refs):
    out_ref, lines, sem = refs[-3:]
    shift = lax.axis_index("vec").astype(jnp.int32) * HALF
    half = (lax.axis_index("gz").astype(jnp.int32) & 1) ^ other
    slots = [
        sum(jnp.where(dirs_ref[o] == mu, o, 0) for o in range(3)).astype(jnp.int32)
        for mu in range(3)
    ]
    places = [jnp.where(half == 0, slots[0], slots[1]), jnp.where(half == 0, 3, slots[2])]
    rows = rows_ref[...]
    copies = []
    for part in range(2):
        near = rows[:, part * 192:(part + 1) * 192]
        far = rows[:, 384 + part * 64:384 + (part + 1) * 64]
        line = jnp.concatenate([near[:, 0:128], far, near[:, 128:192]], 1) * scale
        line = pltpu.roll(line, shift, 1)
        for which in range(2):
            lines[which, part] = line[which * NV:(which + 1) * NV]
            copy = pltpu.make_async_copy(
                lines.at[which, part], out_ref.at[places[which], part], sem.at[which, part]
            )
            copy.start()
            copies.append(copy)
    for copy in copies:
        copy.wait()


def finish(directions, rows, scale, so_far=None):
    other = so_far is not None
    return pl.pallas_call(
        functools.partial(finish_kernel, scale, int(other)),
        out_shape=shape((4, 2, NV, 256), F32),
        in_specs=[SMEM, VMEM] + [HBM] * other,
        out_specs=HBM,
        input_output_aliases={2: 0} if other else {},
        scratch_shapes=[pltpu.VMEM((2, 2, NV, 256), F32), pltpu.SemaphoreType.DMA((2, 2))],
        compiler_params=params(4),
        cost_estimate=pl.CostEstimate(flops=200000, bytes_accessed=1000000, transcendentals=0),
        name="finish_other" if other else "finish_mine",
    )(directions, rows, *([so_far] if other else []))


def permuted(value, axis, target):
    size = lax.axis_size(axis)
    return lax.ppermute(value, axis, [(source, target(source)) for source in range(size)])


def crossed(value, flip, turn):
    pairs = []
    for gz in range(4):
        for gy in range(8):
            x, z = gy % 4, (gy // 4) * 2 + gz // 2
            if gz % 2 == turn:
                x ^= flip
            else:
                z ^= flip
            pairs.append((gz * 8 + gy, ((z % 2) * 2 + gz % 2) * 8 + (z // 2) * 4 + x))
    return lax.ppermute(value, ("gz", "gy"), pairs)


def four_sum(own, opposite, side, other):
    pair = side.astype(F32) + other.astype(F32)
    return pair + (own.astype(F32) + opposite.astype(F32))


def body(vectors, links, momentum, directions):
    rows = vectors.reshape(NV * NK, LANES)
    link_rows = links.reshape(27 * NZY, LANES)
    mid = NV * NK // 2
    prev = permuted(rows, "vec", lambda s: (s + 1) % 4)
    next_ = permuted(rows, "vec", lambda s: (s - 1) % 4)

    y0, y1, z0, z1 = prepare(rows, link_rows)
    yp = permuted(y0, "gy", lambda s: (s - 1) % 8)
    ym = permuted(y1, "gy", lambda s: (s + 1) % 8)
    zp = permuted(z0, "gz", lambda s: (s - 1) % 4)
    z1, zp = lax.optimization_barrier((z1, zp))
    zm = permuted(z1, "gz", lambda s: (s + 1) % 4)
    partial = local_terms(momentum, rows, link_rows)

    far_low = permuted(prev[:mid], "vec", lambda s: (s + 1) % 4)
    far_high = permuted(next_[mid:], "vec", lambda s: (s - 1) % 4)

    right = right_side([rows, next_, prev])
    zm, right = lax.optimization_barrier((zm, right))
    partial = border_terms(2, *partial, zp, zm)
    w = border_terms(1, *partial, yp, ym)[0]

    mate = lambda v: permuted(v, "gz", lambda s: s ^ 1)

    def chip_sum(keep, send):
        return (keep + mate(send)).astype(BF16)

    near = chip_sum(*contract_near(w, right))
    far = chip_sum(*contract_far(w, [far_low, far_high]))
    chip = jnp.concatenate([near, far], 1)
    row = four_sum(chip, *[crossed(chip, flip, 0) for flip in (2, 1, 3)]).astype(BF16)
    plane = four_sum(row, *[crossed(row, flip, 1) for flip in (2, 1, 3)])
    scale = 1.0 / math.sqrt(EXT_X * EXT_Y * EXT_Z)
    mine = finish(directions, plane, scale)
    return finish(directions, mate(plane), scale, mine)


def solution(mesh):
    in_specs = (P("vec", None, "gz", "gy", None), P(None, None, None, "gz", "gy", None), P(), P())
    out_specs = P(None, None, "vec", None)
    return jax.shard_map(body, mesh=mesh, in_specs=in_specs, out_specs=out_specs, check_vma=False)
```

```python
import functools
import math

import jax
import jax.numpy as jnp
from jax import lax
from jax.experimental import pallas as pl
from jax.experimental.pallas import tpu as pltpu
from jax.sharding import PartitionSpec as P

F32 = jnp.float32
BF16 = jnp.bfloat16
VMEM = pl.BlockSpec(memory_space=pltpu.VMEM)
SMEM = pl.BlockSpec(memory_space=pltpu.SMEM)
ANY = pl.BlockSpec(memory_space=pl.ANY)
HBM = pl.BlockSpec(memory_space=pltpu.HBM)

NV = 64
COL = 3
DZ = 8
HY = 2
LANES = 128
HALF = 64
NZY = DZ * HY
EXT_X, EXT_Y, EXT_Z = 64, 16, 32
NK = COL * NZY
KDIM = NK * LANES


def params(limit):
    return pltpu.CompilerParams(vmem_limit_bytes=limit * 1024 * 1024)


def shape(dims, dtype):
    return jax.ShapeDtypeStruct(dims, dtype)


def fetch(sources, targets, sem):
    copies = [
        pltpu.make_async_copy(source, target, sem.at[i])
        for i, (source, target) in enumerate(zip(sources, targets))
    ]
    for copy in copies:
        copy.start()
    return copies


def prepare_kernel(rows, lrows, y0_ref, y1_ref, z0_ref, z1_ref, wide, lwide):
    wide[...] = rows[...].astype(F32)
    lwide[0:432, :] = lrows[...].astype(F32)
    lwide[432:576, :] = jnp.zeros((144, LANES), F32)
    for k in range(NK):
        tile = wide[pl.ds(k, NV, stride=NK), :].astype(BF16)
        c, z, y = k // NZY, (k % NZY) // HY, k % HY
        if y == 0:
            y0_ref[c * DZ + z] = tile
        else:
            y1_ref[c * DZ + z] = tile
        if z == 0:
            z0_ref[c * HY + y] = tile
        if z == DZ - 1:
            z1_ref[c * HY + y] = tile
    rim = lwide[pl.ds(9 * NZY + 1, 72, stride=HY), :]
    rim = jnp.concatenate([rim, jnp.zeros((56, LANES), F32)], 0).astype(BF16)
    y1_ref[24] = rim[0:64]
    y1_ref[25] = rim[64:128]
    low = lwide[pl.ds(18 * NZY + 14, 16, stride=NZY), :]
    high = lwide[pl.ds(18 * NZY + 15, 16, stride=NZY), :]
    rest = jnp.zeros((32, LANES), F32)
    z1_ref[6] = jnp.concatenate([low, high, rest], 0).astype(BF16)


def prepare(rows, link_rows):
    return pl.pallas_call(
        prepare_kernel,
        out_shape=(
            shape((24, NV, LANES), BF16),
            shape((26, NV, LANES), BF16),
            shape((6, NV, LANES), BF16),
            shape((7, NV, LANES), BF16),
        ),
        in_specs=[VMEM] * 2,
        out_specs=(VMEM,) * 4,
        scratch_shapes=[
            pltpu.VMEM((NV * NK, LANES), F32),
            pltpu.VMEM((576, LANES), F32),
        ],
        compiler_params=params(6),
        cost_estimate=pl.CostEstimate(flops=2000000000, bytes_accessed=3000000, transcendentals=0),
        name="prepare",
    )(rows, link_rows)


def line_coefficients(rows, first):
    half = rows * 0.5
    swapped = pltpu.roll(half, HALF, 1)
    return jnp.where(first, half, swapped), jnp.where(first, swapped, half)


def lane_masks():
    lane = lax.broadcasted_iota(jnp.int32, (1, LANES), 1)
    return lane, lane < HALF, jnp.where(lane < HALF, -1.0, 1.0).astype(F32)


def derivative(mu, neighbour, tables, zy, store):
    upr, upi, dnr, dni = tables
    out = [None] * 3
    for c in range(COL):
        here, swap = neighbour(c, 1)
        for r in range(3):
            at = mu * 9 + r * 3 + c
            term = here * upr[zy, at:at + 1, :] + swap * upi[zy, at:at + 1, :]
            out[r] = term if out[r] is None else out[r] + term
    for c in range(COL):
        here, swap = neighbour(c, -1)
        for r in range(3):
            at = mu * 9 + c * 3 + r
            term = here * dnr[zy, at:at + 1, :] - swap * dni[zy, at:at + 1, :]
            out[r] = out[r] - term
    for r in range(3):
        store(r, out[r].astype(BF16))


def local_kernel(
    momentum_ref, v_ref, l_ref, w_ref, ext, exts, upr, upi, dnr, dni,
    wide, lwide, real, imag, cos_ref, sin_ref,
):
    lane, first, sign = lane_masks()
    at = lax.broadcasted_iota(jnp.int32, (NZY, LANES), 0)
    x = lax.broadcasted_iota(jnp.int32, (NZY, LANES), 1) & (HALF - 1)
    y = lax.axis_index("gy").astype(jnp.int32) * HY + (at & (HY - 1))
    z = lax.axis_index("gz").astype(jnp.int32) * DZ + (at >> 1)
    frac_x = ((momentum_ref[0] * x) & (EXT_X - 1)).astype(F32) / EXT_X
    frac_y = ((momentum_ref[1] * y) & (EXT_Y - 1)).astype(F32) / EXT_Y
    frac_z = ((momentum_ref[2] * z) & (EXT_Z - 1)).astype(F32) / EXT_Z
    angle = 2.0 * math.pi * (frac_z + frac_y + frac_x)
    cos_ref[0:NZY, :] = jnp.cos(angle)
    sin_ref[0:NZY, :] = -sign * jnp.sin(angle)

    wide[...] = v_ref[...].astype(F32)
    for c in range(COL):
        for z in range(DZ):
            for y in range(HY):
                tile = wide[pl.ds((c * DZ + z) * HY + y, NV, stride=NK), :]
                ext[c, z + 1, y + 1] = tile
                exts[c, z + 1, y + 1] = pltpu.roll(tile, HALF, 1)

    lwide[0:432, :] = l_ref[...].astype(F32)
    lwide[432:LINES, :] = jnp.zeros((LINES - 432, LANES), F32)
    re, im = line_coefficients(lwide[...], first)
    real[...] = re
    imag[...] = im
    for zy in range(NZY):
        z, y = zy // HY, zy % HY
        pick = pl.ds(zy, 27, stride=NZY)
        upr[zy, 0:27, :] = real[pick, :]
        upi[zy, 0:27, :] = imag[pick, :] * sign
        pick = pl.ds(zy, 9, stride=NZY)
        dnr[zy, 0:9, :] = pltpu.roll(real[pick, :], 1, 1)
        dni[zy, 0:9, :] = pltpu.roll(imag[pick, :], 1, 1) * sign
        if y:
            pick = pl.ds(9 * NZY + zy - 1, 9, stride=NZY)
            dnr[zy, 9:18, :] = real[pick, :]
            dni[zy, 9:18, :] = imag[pick, :] * sign
        if z:
            pick = pl.ds(18 * NZY + zy - HY, 9, stride=NZY)
            dnr[zy, 18:27, :] = real[pick, :]
            dni[zy, 18:27, :] = imag[pick, :] * sign

    wrap_up = (lane == HALF - 1) | (lane == LANES - 1)
    wrap_down = (lane == 0) | (lane == HALF)

    def site(zy, carry):
        z = lax.div(zy, HY) + 1
        y = lax.rem(zy, HY) + 1

        def neighbour(c, step):
            here, swap = ext[c, z, y], exts[c, z, y]
            a = pltpu.roll(here, (-step) % LANES, 1)
            b = pltpu.roll(swap, (-step) % LANES, 1)
            wrap = wrap_up if step == 1 else wrap_down
            return jnp.where(wrap, b, a), jnp.where(wrap, a, b)

        def store(r, value):
            column = pl.multiple_of((r * NZY + zy) * LANES, LANES)
            w_ref[0, :, pl.ds(column, LANES)] = value

        derivative(0, neighbour, (upr, upi, dnr, dni), zy, store)
        cosine = cos_ref[pl.ds(zy, 1), :]
        sine = sin_ref[pl.ds(zy, 1), :]
        for c in range(COL):
            column = pl.multiple_of((c * NZY + zy) * LANES, LANES)
            phased = ext[c, z, y] * cosine + exts[c, z, y] * sine
            w_ref[1, :, pl.ds(column, LANES)] = phased.astype(BF16)
        return carry

    lax.fori_loop(0, NZY, site, 0)


EXTENDED = (COL, DZ + 2, HY + 2, NV, LANES)
TABLE = (NZY, 40, LANES)
LINES = 576


def local_terms(momentum, rows, link_rows):
    line = pltpu.VMEM((LINES, LANES), F32)
    return pl.pallas_call(
        local_kernel,
        out_shape=(shape((4, NV, KDIM), BF16),)
        + (shape(EXTENDED, F32),) * 2
        + (shape(TABLE, F32),) * 4,
        in_specs=[SMEM] + [VMEM] * 2,
        out_specs=(VMEM,) * 7,
        scratch_shapes=[
            pltpu.VMEM((NV * NK, LANES), F32),
            line,
            line,
            line,
            pltpu.VMEM((NZY + 8, LANES), F32),
            pltpu.VMEM((NZY + 8, LANES), F32),
        ],
        compiler_params=params(8),
        cost_estimate=pl.CostEstimate(flops=6000000000, bytes_accessed=6000000, transcendentals=0),
        name="local_terms",
    )(momentum, rows, link_rows)


def border_kernel(
    mu, before_ref, e_ref, s_ref, upr, upi, r_ref, i_ref, ahead_ref, behind_ref,
    w_ref, ext, exts, dnr, dni, lwide, real, imag,
):
    lane, first, sign = lane_masks()

    def put(c, z, y, tile):
        tile = tile.astype(F32)
        ext[c, z, y] = tile
        exts[c, z, y] = pltpu.roll(tile, HALF, 1)

    for c in range(COL):
        if mu == 1:
            for z in range(DZ):
                put(c, z + 1, HY + 1, ahead_ref[c * DZ + z])
                put(c, z + 1, 0, behind_ref[c * DZ + z])
        else:
            for y in range(HY):
                put(c, DZ + 1, y + 1, ahead_ref[c * HY + y])
                put(c, 0, y + 1, behind_ref[c * HY + y])

    if mu == 1:
        lwide[...] = jnp.concatenate([behind_ref[24], behind_ref[25]], 0).astype(F32)
    else:
        lwide[0:64, :] = behind_ref[6].astype(F32)
        lwide[64:128, :] = jnp.zeros((64, LANES), F32)
    re, im = line_coefficients(lwide[...], first)
    real[...] = re
    imag[...] = im * sign
    if mu == 1:
        for z in range(DZ):
            pick = pl.ds(z, 9, stride=DZ)
            dnr[z * HY, 9:18, :] = real[pick, :]
            dni[z * HY, 9:18, :] = imag[pick, :]
    else:
        for y in range(HY):
            pick = pl.ds(16 * y, 9)
            dnr[y, 18:27, :] = real[pick, :]
            dni[y, 18:27, :] = imag[pick, :]

    def site(zy, carry):
        z = lax.div(zy, HY) + 1
        y = lax.rem(zy, HY) + 1

        def neighbour(c, step):
            at = (c, z, y + step) if mu == 1 else (c, z + step, y)
            return ext[at], exts[at]

        def store(r, value):
            column = pl.multiple_of((r * NZY + zy) * LANES, LANES)
            w_ref[mu + 1, :, pl.ds(column, LANES)] = value

        derivative(mu, neighbour, (upr, upi, dnr, dni), zy, store)
        return carry

    lax.fori_loop(0, NZY, site, 0)


def border_terms(mu, w, ext, exts, upr, upi, dnr, dni, ahead, behind):
    line = pltpu.VMEM((128, LANES), F32)
    w, ext, exts, dnr, dni = pl.pallas_call(
        functools.partial(border_kernel, mu),
        out_shape=(shape((4, NV, KDIM), BF16),)
        + (shape(EXTENDED, F32),) * 2
        + (shape(TABLE, F32),) * 2,
        in_specs=[VMEM] * 9,
        out_specs=(VMEM,) * 5,
        input_output_aliases={0: 0, 1: 1, 2: 2, 5: 3, 6: 4},
        scratch_shapes=[line, line, line],
        compiler_params=params(4),
        cost_estimate=pl.CostEstimate(flops=3000000000, bytes_accessed=3000000, transcendentals=0),
        name="border_y" if mu == 1 else "border_z",
    )(w, ext, exts, upr, upi, dnr, dni, ahead, behind)
    return w, ext, exts, upr, upi, dnr, dni


def fill_right(counts, blocks, wide, right):
    total = sum(counts)
    lane, first, sign = lane_masks()
    start = 0
    for block, count in zip(blocks, counts):
        wide[0:count * NK, :] = block[...].astype(F32)
        for k in range(NK):
            tile = wide[pl.ds(k, count, stride=NK), :]
            swap = pltpu.roll(tile, HALF, 1) * sign
            right[start:start + count, k * LANES:(k + 1) * LANES] = tile.astype(BF16)
            right[total + start:total + start + count, k * LANES:(k + 1) * LANES] = swap.astype(BF16)
        start += count


def dot_halves(w_ref, right, keep_ref, send_ref, product):
    left = w_ref[...].reshape(4 * NV, KDIM)
    dots = lax.dot_general(left, right[...], (((1,), (1,)), ((), ())), preferred_element_type=F32)
    product[...] = dots.reshape(2, 2 * NV, dots.shape[1])
    mine = lax.axis_index("gz").astype(jnp.int32) & 1
    keep_ref[...] = product[mine]
    send_ref[...] = product[1 - mine]


def right_kernel(counts, *refs):
    n = len(counts)
    fill_right(counts, refs[:n], refs[n + 1], refs[n])


def right_side(blocks):
    counts = tuple(b.shape[0] // NK for b in blocks)
    return pl.pallas_call(
        functools.partial(right_kernel, counts),
        out_shape=shape((2 * sum(counts), KDIM), BF16),
        in_specs=[VMEM] * len(blocks),
        out_specs=VMEM,
        scratch_shapes=[pltpu.VMEM((max(counts) * NK, LANES), F32)],
        compiler_params=params(4),
        cost_estimate=pl.CostEstimate(flops=2000000000, bytes_accessed=4000000, transcendentals=0),
        name="right_side",
    )(*blocks)


def near_kernel(w_ref, right_ref, keep_ref, send_ref, product):
    dot_halves(w_ref, right_ref, keep_ref, send_ref, product)


def far_kernel(counts, w_ref, *refs):
    n = len(counts)
    keep_ref, send_ref, wide, right, product = refs[n:]
    fill_right(counts, refs[:n], wide, right)
    dot_halves(w_ref, right, keep_ref, send_ref, product)


def contract_near(w, right):
    columns = right.shape[0]
    out = shape((2 * NV, columns), F32)
    return pl.pallas_call(
        near_kernel,
        out_shape=(out, out),
        in_specs=[VMEM] * 2,
        out_specs=(VMEM, VMEM),
        scratch_shapes=[pltpu.VMEM((2, 2 * NV, columns), F32)],
        compiler_params=params(4),
        cost_estimate=pl.CostEstimate(
            flops=2 * 256 * columns * KDIM, bytes_accessed=4000000, transcendentals=0
        ),
        name="contract_near",
    )(w, right)


def contract_far(w, blocks):
    counts = tuple(b.shape[0] // NK for b in blocks)
    columns = 2 * sum(counts)
    out = shape((2 * NV, columns), F32)
    return pl.pallas_call(
        functools.partial(far_kernel, counts),
        out_shape=(out, out),
        in_specs=[VMEM] * (1 + len(blocks)),
        out_specs=(VMEM, VMEM),
        scratch_shapes=[
            pltpu.VMEM((max(counts) * NK, LANES), F32),
            pltpu.VMEM((columns, KDIM), BF16),
            pltpu.VMEM((2, 2 * NV, columns), F32),
        ],
        compiler_params=params(5),
        cost_estimate=pl.CostEstimate(
            flops=2 * 256 * columns * KDIM, bytes_accessed=4000000, transcendentals=0
        ),
        name="contract_far",
    )(w, *blocks)


def finish_kernel(scale, other, dirs_ref, rows_ref, *refs):
    out_ref, lines, sem = refs[-3:]
    shift = lax.axis_index("vec").astype(jnp.int32) * HALF
    half = (lax.axis_index("gz").astype(jnp.int32) & 1) ^ other
    slots = [
        sum(jnp.where(dirs_ref[o] == mu, o, 0) for o in range(3)).astype(jnp.int32)
        for mu in range(3)
    ]
    places = [jnp.where(half == 0, slots[0], slots[1]), jnp.where(half == 0, 3, slots[2])]
    rows = rows_ref[...]
    copies = []
    for part in range(2):
        near = rows[:, part * 192:(part + 1) * 192]
        far = rows[:, 384 + part * 64:384 + (part + 1) * 64]
        line = jnp.concatenate([near[:, 0:128], far, near[:, 128:192]], 1) * scale
        line = pltpu.roll(line, shift, 1)
        for which in range(2):
            lines[which, part] = line[which * NV:(which + 1) * NV]
            copy = pltpu.make_async_copy(
                lines.at[which, part], out_ref.at[places[which], part], sem.at[which, part]
            )
            copy.start()
            copies.append(copy)
    for copy in copies:
        copy.wait()


def finish(directions, rows, scale, so_far=None):
    other = so_far is not None
    return pl.pallas_call(
        functools.partial(finish_kernel, scale, int(other)),
        out_shape=shape((4, 2, NV, 256), F32),
        in_specs=[SMEM, VMEM] + [HBM] * other,
        out_specs=HBM,
        input_output_aliases={2: 0} if other else {},
        scratch_shapes=[pltpu.VMEM((2, 2, NV, 256), F32), pltpu.SemaphoreType.DMA((2, 2))],
        compiler_params=params(4),
        cost_estimate=pl.CostEstimate(flops=200000, bytes_accessed=1000000, transcendentals=0),
        name="finish_other" if other else "finish_mine",
    )(directions, rows, *([so_far] if other else []))


def permuted(value, axis, target):
    size = lax.axis_size(axis)
    return lax.ppermute(value, axis, [(source, target(source)) for source in range(size)])


def crossed(value, flip, turn):
    pairs = []
    for gz in range(4):
        for gy in range(8):
            x, z = gy % 4, (gy // 4) * 2 + gz // 2
            if gz % 2 == turn:
                x ^= flip
            else:
                z ^= flip
            pairs.append((gz * 8 + gy, ((z % 2) * 2 + gz % 2) * 8 + (z // 2) * 4 + x))
    return lax.ppermute(value, ("gz", "gy"), pairs)


def four_sum(own, opposite, side, other):
    pair = side.astype(F32) + other.astype(F32)
    return pair + (own.astype(F32) + opposite.astype(F32))


def body(vectors, links, momentum, directions):
    rows = vectors.reshape(NV * NK, LANES)
    link_rows = links.reshape(27 * NZY, LANES)
    mid = NV * NK // 2
    prev = permuted(rows, "vec", lambda s: (s + 1) % 4)
    next_ = permuted(rows, "vec", lambda s: (s - 1) % 4)

    y0, y1, z0, z1 = prepare(rows, link_rows)
    yp = permuted(y0, "gy", lambda s: (s - 1) % 8)
    ym = permuted(y1, "gy", lambda s: (s + 1) % 8)
    zp = permuted(z0, "gz", lambda s: (s - 1) % 4)
    z1, zp = lax.optimization_barrier((z1, zp))
    zm = permuted(z1, "gz", lambda s: (s + 1) % 4)
    partial = local_terms(momentum, rows, link_rows)

    far_low = permuted(prev[:mid], "vec", lambda s: (s + 1) % 4)
    far_high = permuted(next_[mid:], "vec", lambda s: (s - 1) % 4)

    right = right_side([rows, next_, prev])
    zm, right = lax.optimization_barrier((zm, right))
    partial = border_terms(2, *partial, zp, zm)
    w = border_terms(1, *partial, yp, ym)[0]

    mate = lambda v: permuted(v, "gz", lambda s: s ^ 1)

    def chip_sum(keep, send):
        return (keep + mate(send)).astype(BF16)

    near = chip_sum(*contract_near(w, right))
    far = chip_sum(*contract_far(w, [far_low, far_high]))
    chip = jnp.concatenate([near, far], 1)
    row = four_sum(chip, *[crossed(chip, flip, 0) for flip in (2, 1, 3)]).astype(BF16)
    plane = four_sum(row, *[crossed(row, flip, 1) for flip in (2, 1, 3)])
    scale = 1.0 / math.sqrt(EXT_X * EXT_Y * EXT_Z)
    mine = finish(directions, plane, scale)
    return finish(directions, mate(plane), scale, mine)


def solution(mesh):
    in_specs = (P("vec", None, "gz", "gy", None), P(None, None, None, "gz", "gy", None), P(), P())
    out_specs = P(None, None, "vec", None)
    return jax.shard_map(body, mesh=mesh, in_specs=in_specs, out_specs=out_specs, check_vma=False)
```

```python
import functools
import math

import jax
import jax.numpy as jnp
from jax import lax
from jax.experimental import pallas as pl
from jax.experimental.pallas import tpu as pltpu
from jax.sharding import PartitionSpec as P

F32 = jnp.float32
BF16 = jnp.bfloat16
VMEM = pl.BlockSpec(memory_space=pltpu.VMEM)
SMEM = pl.BlockSpec(memory_space=pltpu.SMEM)
ANY = pl.BlockSpec(memory_space=pl.ANY)
HBM = pl.BlockSpec(memory_space=pltpu.HBM)

NV = 64
COL = 3
DZ = 8
HY = 2
LANES = 128
HALF = 64
NZY = DZ * HY
EXT_X, EXT_Y, EXT_Z = 64, 16, 32
NK = COL * NZY
KDIM = NK * LANES


def params(limit):
    return pltpu.CompilerParams(vmem_limit_bytes=limit * 1024 * 1024)


def shape(dims, dtype):
    return jax.ShapeDtypeStruct(dims, dtype)


def fetch(sources, targets, sem):
    copies = [
        pltpu.make_async_copy(source, target, sem.at[i])
        for i, (source, target) in enumerate(zip(sources, targets))
    ]
    for copy in copies:
        copy.start()
    return copies


def prepare_kernel(rows, lrows, y0_ref, y1_ref, z0_ref, z1_ref, wide, lwide):
    wide[...] = rows[...].astype(F32)
    lwide[0:432, :] = lrows[...].astype(F32)
    lwide[432:576, :] = jnp.zeros((144, LANES), F32)
    for k in range(NK):
        tile = wide[pl.ds(k, NV, stride=NK), :].astype(BF16)
        c, z, y = k // NZY, (k % NZY) // HY, k % HY
        if y == 0:
            y0_ref[c * DZ + z] = tile
        else:
            y1_ref[c * DZ + z] = tile
        if z == 0:
            z0_ref[c * HY + y] = tile
        if z == DZ - 1:
            z1_ref[c * HY + y] = tile
    rim = lwide[pl.ds(9 * NZY + 1, 72, stride=HY), :]
    rim = jnp.concatenate([rim, jnp.zeros((56, LANES), F32)], 0).astype(BF16)
    y1_ref[24] = rim[0:64]
    y1_ref[25] = rim[64:128]
    low = lwide[pl.ds(18 * NZY + 14, 16, stride=NZY), :]
    high = lwide[pl.ds(18 * NZY + 15, 16, stride=NZY), :]
    rest = jnp.zeros((32, LANES), F32)
    z1_ref[6] = jnp.concatenate([low, high, rest], 0).astype(BF16)


def prepare(rows, link_rows):
    return pl.pallas_call(
        prepare_kernel,
        out_shape=(
            shape((24, NV, LANES), BF16),
            shape((26, NV, LANES), BF16),
            shape((6, NV, LANES), BF16),
            shape((7, NV, LANES), BF16),
        ),
        in_specs=[VMEM] * 2,
        out_specs=(VMEM,) * 4,
        scratch_shapes=[
            pltpu.VMEM((NV * NK, LANES), F32),
            pltpu.VMEM((576, LANES), F32),
        ],
        compiler_params=params(6),
        cost_estimate=pl.CostEstimate(flops=2000000000, bytes_accessed=3000000, transcendentals=0),
        name="prepare",
    )(rows, link_rows)


def line_coefficients(rows, first):
    half = rows * 0.5
    swapped = pltpu.roll(half, HALF, 1)
    return jnp.where(first, half, swapped), jnp.where(first, swapped, half)


def lane_masks():
    lane = lax.broadcasted_iota(jnp.int32, (1, LANES), 1)
    return lane, lane < HALF, jnp.where(lane < HALF, -1.0, 1.0).astype(F32)


def derivative(mu, neighbour, tables, zy, store):
    upr, upi, dnr, dni = tables
    out = [None] * 3
    for c in range(COL):
        here, swap = neighbour(c, 1)
        for r in range(3):
            at = mu * 9 + r * 3 + c
            term = here * upr[zy, at:at + 1, :] + swap * upi[zy, at:at + 1, :]
            out[r] = term if out[r] is None else out[r] + term
    for c in range(COL):
        here, swap = neighbour(c, -1)
        for r in range(3):
            at = mu * 9 + c * 3 + r
            term = here * dnr[zy, at:at + 1, :] - swap * dni[zy, at:at + 1, :]
            out[r] = out[r] - term
    for r in range(3):
        store(r, out[r].astype(BF16))


def local_kernel(
    momentum_ref, v_ref, l_ref, w_ref, ext, exts, upr, upi, dnr, dni,
    wide, lwide, real, imag, cos_ref, sin_ref,
):
    lane, first, sign = lane_masks()
    at = lax.broadcasted_iota(jnp.int32, (NZY, LANES), 0)
    x = lax.broadcasted_iota(jnp.int32, (NZY, LANES), 1) & (HALF - 1)
    y = lax.axis_index("gy").astype(jnp.int32) * HY + (at & (HY - 1))
    z = lax.axis_index("gz").astype(jnp.int32) * DZ + (at >> 1)
    frac_x = ((momentum_ref[0] * x) & (EXT_X - 1)).astype(F32) / EXT_X
    frac_y = ((momentum_ref[1] * y) & (EXT_Y - 1)).astype(F32) / EXT_Y
    frac_z = ((momentum_ref[2] * z) & (EXT_Z - 1)).astype(F32) / EXT_Z
    angle = 2.0 * math.pi * (frac_z + frac_y + frac_x)
    cos_ref[0:NZY, :] = jnp.cos(angle)
    sin_ref[0:NZY, :] = -sign * jnp.sin(angle)

    wide[...] = v_ref[...].astype(F32)
    for c in range(COL):
        for z in range(DZ):
            for y in range(HY):
                tile = wide[pl.ds((c * DZ + z) * HY + y, NV, stride=NK), :]
                ext[c, z + 1, y + 1] = tile
                exts[c, z + 1, y + 1] = pltpu.roll(tile, HALF, 1)

    lwide[0:432, :] = l_ref[...].astype(F32)
    lwide[432:LINES, :] = jnp.zeros((LINES - 432, LANES), F32)
    re, im = line_coefficients(lwide[...], first)
    real[...] = re
    imag[...] = im
    for zy in range(NZY):
        z, y = zy // HY, zy % HY
        pick = pl.ds(zy, 27, stride=NZY)
        upr[zy, 0:27, :] = real[pick, :]
        upi[zy, 0:27, :] = imag[pick, :] * sign
        pick = pl.ds(zy, 9, stride=NZY)
        dnr[zy, 0:9, :] = pltpu.roll(real[pick, :], 1, 1)
        dni[zy, 0:9, :] = pltpu.roll(imag[pick, :], 1, 1) * sign
        if y:
            pick = pl.ds(9 * NZY + zy - 1, 9, stride=NZY)
            dnr[zy, 9:18, :] = real[pick, :]
            dni[zy, 9:18, :] = imag[pick, :] * sign
        if z:
            pick = pl.ds(18 * NZY + zy - HY, 9, stride=NZY)
            dnr[zy, 18:27, :] = real[pick, :]
            dni[zy, 18:27, :] = imag[pick, :] * sign

    wrap_up = (lane == HALF - 1) | (lane == LANES - 1)
    wrap_down = (lane == 0) | (lane == HALF)

    def site(zy, carry):
        z = lax.div(zy, HY) + 1
        y = lax.rem(zy, HY) + 1

        def neighbour(c, step):
            here, swap = ext[c, z, y], exts[c, z, y]
            a = pltpu.roll(here, (-step) % LANES, 1)
            b = pltpu.roll(swap, (-step) % LANES, 1)
            wrap = wrap_up if step == 1 else wrap_down
            return jnp.where(wrap, b, a), jnp.where(wrap, a, b)

        def store(r, value):
            column = pl.multiple_of((r * NZY + zy) * LANES, LANES)
            w_ref[0, :, pl.ds(column, LANES)] = value

        derivative(0, neighbour, (upr, upi, dnr, dni), zy, store)
        cosine = cos_ref[pl.ds(zy, 1), :]
        sine = sin_ref[pl.ds(zy, 1), :]
        for c in range(COL):
            column = pl.multiple_of((c * NZY + zy) * LANES, LANES)
            phased = ext[c, z, y] * cosine + exts[c, z, y] * sine
            w_ref[1, :, pl.ds(column, LANES)] = phased.astype(BF16)
        return carry

    lax.fori_loop(0, NZY, site, 0, unroll=2)


EXTENDED = (COL, DZ + 2, HY + 2, NV, LANES)
TABLE = (NZY, 40, LANES)
LINES = 576


def local_terms(momentum, rows, link_rows):
    line = pltpu.VMEM((LINES, LANES), F32)
    return pl.pallas_call(
        local_kernel,
        out_shape=(shape((4, NV, KDIM), BF16),)
        + (shape(EXTENDED, F32),) * 2
        + (shape(TABLE, F32),) * 4,
        in_specs=[SMEM] + [VMEM] * 2,
        out_specs=(VMEM,) * 7,
        scratch_shapes=[
            pltpu.VMEM((NV * NK, LANES), F32),
            line,
            line,
            line,
            pltpu.VMEM((NZY + 8, LANES), F32),
            pltpu.VMEM((NZY + 8, LANES), F32),
        ],
        compiler_params=params(8),
        cost_estimate=pl.CostEstimate(flops=6000000000, bytes_accessed=6000000, transcendentals=0),
        name="local_terms",
    )(momentum, rows, link_rows)


def border_kernel(
    mu, before_ref, e_ref, s_ref, upr, upi, r_ref, i_ref, ahead_ref, behind_ref,
    w_ref, ext, exts, dnr, dni, lwide, real, imag,
):
    lane, first, sign = lane_masks()

    def put(c, z, y, tile):
        tile = tile.astype(F32)
        ext[c, z, y] = tile
        exts[c, z, y] = pltpu.roll(tile, HALF, 1)

    for c in range(COL):
        if mu == 1:
            for z in range(DZ):
                put(c, z + 1, HY + 1, ahead_ref[c * DZ + z])
                put(c, z + 1, 0, behind_ref[c * DZ + z])
        else:
            for y in range(HY):
                put(c, DZ + 1, y + 1, ahead_ref[c * HY + y])
                put(c, 0, y + 1, behind_ref[c * HY + y])

    if mu == 1:
        lwide[...] = jnp.concatenate([behind_ref[24], behind_ref[25]], 0).astype(F32)
    else:
        lwide[0:64, :] = behind_ref[6].astype(F32)
        lwide[64:128, :] = jnp.zeros((64, LANES), F32)
    re, im = line_coefficients(lwide[...], first)
    real[...] = re
    imag[...] = im * sign
    if mu == 1:
        for z in range(DZ):
            pick = pl.ds(z, 9, stride=DZ)
            dnr[z * HY, 9:18, :] = real[pick, :]
            dni[z * HY, 9:18, :] = imag[pick, :]
    else:
        for y in range(HY):
            pick = pl.ds(16 * y, 9)
            dnr[y, 18:27, :] = real[pick, :]
            dni[y, 18:27, :] = imag[pick, :]

    def site(zy, carry):
        z = lax.div(zy, HY) + 1
        y = lax.rem(zy, HY) + 1

        def neighbour(c, step):
            at = (c, z, y + step) if mu == 1 else (c, z + step, y)
            return ext[at], exts[at]

        def store(r, value):
            column = pl.multiple_of((r * NZY + zy) * LANES, LANES)
            w_ref[mu + 1, :, pl.ds(column, LANES)] = value

        derivative(mu, neighbour, (upr, upi, dnr, dni), zy, store)
        return carry

    lax.fori_loop(0, NZY, site, 0, unroll=2)


def border_terms(mu, w, ext, exts, upr, upi, dnr, dni, ahead, behind):
    line = pltpu.VMEM((128, LANES), F32)
    w, ext, exts, dnr, dni = pl.pallas_call(
        functools.partial(border_kernel, mu),
        out_shape=(shape((4, NV, KDIM), BF16),)
        + (shape(EXTENDED, F32),) * 2
        + (shape(TABLE, F32),) * 2,
        in_specs=[VMEM] * 9,
        out_specs=(VMEM,) * 5,
        input_output_aliases={0: 0, 1: 1, 2: 2, 5: 3, 6: 4},
        scratch_shapes=[line, line, line],
        compiler_params=params(4),
        cost_estimate=pl.CostEstimate(flops=3000000000, bytes_accessed=3000000, transcendentals=0),
        name="border_y" if mu == 1 else "border_z",
    )(w, ext, exts, upr, upi, dnr, dni, ahead, behind)
    return w, ext, exts, upr, upi, dnr, dni


def fill_right(counts, blocks, wide, right):
    total = sum(counts)
    lane, first, sign = lane_masks()
    start = 0
    for block, count in zip(blocks, counts):
        wide[0:count * NK, :] = block[...].astype(F32)
        for k in range(NK):
            tile = wide[pl.ds(k, count, stride=NK), :]
            swap = pltpu.roll(tile, HALF, 1) * sign
            right[start:start + count, k * LANES:(k + 1) * LANES] = tile.astype(BF16)
            right[total + start:total + start + count, k * LANES:(k + 1) * LANES] = swap.astype(BF16)
        start += count


def dot_halves(w_ref, right, keep_ref, send_ref, product):
    left = w_ref[...].reshape(4 * NV, KDIM)
    dots = lax.dot_general(left, right[...], (((1,), (1,)), ((), ())), preferred_element_type=F32)
    product[...] = dots.reshape(2, 2 * NV, dots.shape[1])
    mine = lax.axis_index("gz").astype(jnp.int32) & 1
    keep_ref[...] = product[mine]
    send_ref[...] = product[1 - mine]


def right_kernel(counts, *refs):
    n = len(counts)
    fill_right(counts, refs[:n], refs[n + 1], refs[n])


def right_side(blocks):
    counts = tuple(b.shape[0] // NK for b in blocks)
    return pl.pallas_call(
        functools.partial(right_kernel, counts),
        out_shape=shape((2 * sum(counts), KDIM), BF16),
        in_specs=[VMEM] * len(blocks),
        out_specs=VMEM,
        scratch_shapes=[pltpu.VMEM((max(counts) * NK, LANES), F32)],
        compiler_params=params(4),
        cost_estimate=pl.CostEstimate(flops=2000000000, bytes_accessed=4000000, transcendentals=0),
        name="right_side",
    )(*blocks)


def near_kernel(w_ref, right_ref, keep_ref, send_ref, product):
    dot_halves(w_ref, right_ref, keep_ref, send_ref, product)


def far_kernel(counts, w_ref, *refs):
    n = len(counts)
    keep_ref, send_ref, wide, right, product = refs[n:]
    fill_right(counts, refs[:n], wide, right)
    dot_halves(w_ref, right, keep_ref, send_ref, product)


def contract_near(w, right):
    columns = right.shape[0]
    out = shape((2 * NV, columns), F32)
    return pl.pallas_call(
        near_kernel,
        out_shape=(out, out),
        in_specs=[VMEM] * 2,
        out_specs=(VMEM, VMEM),
        scratch_shapes=[pltpu.VMEM((2, 2 * NV, columns), F32)],
        compiler_params=params(4),
        cost_estimate=pl.CostEstimate(
            flops=2 * 256 * columns * KDIM, bytes_accessed=4000000, transcendentals=0
        ),
        name="contract_near",
    )(w, right)


def contract_far(w, blocks):
    counts = tuple(b.shape[0] // NK for b in blocks)
    columns = 2 * sum(counts)
    out = shape((2 * NV, columns), F32)
    return pl.pallas_call(
        functools.partial(far_kernel, counts),
        out_shape=(out, out),
        in_specs=[VMEM] * (1 + len(blocks)),
        out_specs=(VMEM, VMEM),
        scratch_shapes=[
            pltpu.VMEM((max(counts) * NK, LANES), F32),
            pltpu.VMEM((columns, KDIM), BF16),
            pltpu.VMEM((2, 2 * NV, columns), F32),
        ],
        compiler_params=params(5),
        cost_estimate=pl.CostEstimate(
            flops=2 * 256 * columns * KDIM, bytes_accessed=4000000, transcendentals=0
        ),
        name="contract_far",
    )(w, *blocks)


def finish_kernel(scale, other, dirs_ref, rows_ref, *refs):
    out_ref, lines, sem = refs[-3:]
    shift = lax.axis_index("vec").astype(jnp.int32) * HALF
    half = (lax.axis_index("gz").astype(jnp.int32) & 1) ^ other
    slots = [
        sum(jnp.where(dirs_ref[o] == mu, o, 0) for o in range(3)).astype(jnp.int32)
        for mu in range(3)
    ]
    places = [jnp.where(half == 0, slots[0], slots[1]), jnp.where(half == 0, 3, slots[2])]
    rows = rows_ref[...]
    copies = []
    for part in range(2):
        near = rows[:, part * 192:(part + 1) * 192]
        far = rows[:, 384 + part * 64:384 + (part + 1) * 64]
        line = jnp.concatenate([near[:, 0:128], far, near[:, 128:192]], 1) * scale
        line = pltpu.roll(line, shift, 1)
        for which in range(2):
            lines[which, part] = line[which * NV:(which + 1) * NV]
            copy = pltpu.make_async_copy(
                lines.at[which, part], out_ref.at[places[which], part], sem.at[which, part]
            )
            copy.start()
            copies.append(copy)
    for copy in copies:
        copy.wait()


def finish(directions, rows, scale, so_far=None):
    other = so_far is not None
    return pl.pallas_call(
        functools.partial(finish_kernel, scale, int(other)),
        out_shape=shape((4, 2, NV, 256), F32),
        in_specs=[SMEM, VMEM] + [HBM] * other,
        out_specs=HBM,
        input_output_aliases={2: 0} if other else {},
        scratch_shapes=[pltpu.VMEM((2, 2, NV, 256), F32), pltpu.SemaphoreType.DMA((2, 2))],
        compiler_params=params(4),
        cost_estimate=pl.CostEstimate(flops=200000, bytes_accessed=1000000, transcendentals=0),
        name="finish_other" if other else "finish_mine",
    )(directions, rows, *([so_far] if other else []))


def permuted(value, axis, target):
    size = lax.axis_size(axis)
    return lax.ppermute(value, axis, [(source, target(source)) for source in range(size)])


def crossed(value, flip, turn):
    pairs = []
    for gz in range(4):
        for gy in range(8):
            x, z = gy % 4, (gy // 4) * 2 + gz // 2
            if gz % 2 == turn:
                x ^= flip
            else:
                z ^= flip
            pairs.append((gz * 8 + gy, ((z % 2) * 2 + gz % 2) * 8 + (z // 2) * 4 + x))
    return lax.ppermute(value, ("gz", "gy"), pairs)


def four_sum(own, opposite, side, other):
    pair = side.astype(F32) + other.astype(F32)
    return pair + (own.astype(F32) + opposite.astype(F32))


def body(vectors, links, momentum, directions):
    rows = vectors.reshape(NV * NK, LANES)
    link_rows = links.reshape(27 * NZY, LANES)
    mid = NV * NK // 2
    prev = permuted(rows, "vec", lambda s: (s + 1) % 4)
    next_ = permuted(rows, "vec", lambda s: (s - 1) % 4)

    y0, y1, z0, z1 = prepare(rows, link_rows)
    yp = permuted(y0, "gy", lambda s: (s - 1) % 8)
    ym = permuted(y1, "gy", lambda s: (s + 1) % 8)
    zp = permuted(z0, "gz", lambda s: (s - 1) % 4)
    z1, zp = lax.optimization_barrier((z1, zp))
    zm = permuted(z1, "gz", lambda s: (s + 1) % 4)
    partial = local_terms(momentum, rows, link_rows)

    far_low = permuted(prev[:mid], "vec", lambda s: (s + 1) % 4)
    far_high = permuted(next_[mid:], "vec", lambda s: (s - 1) % 4)

    right = right_side([rows, next_, prev])
    zm, right = lax.optimization_barrier((zm, right))
    partial = border_terms(2, *partial, zp, zm)
    w = border_terms(1, *partial, yp, ym)[0]

    mate = lambda v: permuted(v, "gz", lambda s: s ^ 1)

    def chip_sum(keep, send):
        return (keep + mate(send)).astype(BF16)

    near = chip_sum(*contract_near(w, right))
    far = chip_sum(*contract_far(w, [far_low, far_high]))
    chip = jnp.concatenate([near, far], 1)
    row = four_sum(chip, *[crossed(chip, flip, 1) for flip in (2, 1, 3)]).astype(BF16)
    plane = four_sum(row, *[crossed(row, flip, 0) for flip in (2, 1, 3)])
    scale = 1.0 / math.sqrt(EXT_X * EXT_Y * EXT_Z)
    mine = finish(directions, plane, scale)
    return finish(directions, mate(plane), scale, mine)


def solution(mesh):
    in_specs = (P("vec", None, "gz", "gy", None), P(None, None, None, "gz", "gy", None), P(), P())
    out_specs = P(None, None, "vec", None)
    return jax.shard_map(body, mesh=mesh, in_specs=in_specs, out_specs=out_specs, check_vma=False)
```

```python
import functools
import math

import jax
import jax.numpy as jnp
from jax import lax
from jax.experimental import pallas as pl
from jax.experimental.pallas import tpu as pltpu
from jax.sharding import PartitionSpec as P

F32 = jnp.float32
BF16 = jnp.bfloat16
VMEM = pl.BlockSpec(memory_space=pltpu.VMEM)
SMEM = pl.BlockSpec(memory_space=pltpu.SMEM)
ANY = pl.BlockSpec(memory_space=pl.ANY)
HBM = pl.BlockSpec(memory_space=pltpu.HBM)

NV = 64
COL = 3
DZ = 8
HY = 2
LANES = 128
HALF = 64
NZY = DZ * HY
EXT_X, EXT_Y, EXT_Z = 64, 16, 32
NK = COL * NZY
KDIM = NK * LANES


def params(limit):
    return pltpu.CompilerParams(vmem_limit_bytes=limit * 1024 * 1024)


def shape(dims, dtype):
    return jax.ShapeDtypeStruct(dims, dtype)


def fetch(sources, targets, sem):
    copies = [
        pltpu.make_async_copy(source, target, sem.at[i])
        for i, (source, target) in enumerate(zip(sources, targets))
    ]
    for copy in copies:
        copy.start()
    return copies


def prepare_kernel(rows, lrows, y0_ref, y1_ref, z0_ref, z1_ref, wide, lwide):
    wide[...] = rows[...].astype(F32)
    lwide[0:432, :] = lrows[...].astype(F32)
    lwide[432:576, :] = jnp.zeros((144, LANES), F32)
    for k in range(NK):
        tile = wide[pl.ds(k, NV, stride=NK), :].astype(BF16)
        c, z, y = k // NZY, (k % NZY) // HY, k % HY
        if y == 0:
            y0_ref[c * DZ + z] = tile
        else:
            y1_ref[c * DZ + z] = tile
        if z == 0:
            z0_ref[c * HY + y] = tile
        if z == DZ - 1:
            z1_ref[c * HY + y] = tile
    rim = lwide[pl.ds(9 * NZY + 1, 72, stride=HY), :]
    rim = jnp.concatenate([rim, jnp.zeros((56, LANES), F32)], 0).astype(BF16)
    y1_ref[24] = rim[0:64]
    y1_ref[25] = rim[64:128]
    low = lwide[pl.ds(18 * NZY + 14, 16, stride=NZY), :]
    high = lwide[pl.ds(18 * NZY + 15, 16, stride=NZY), :]
    rest = jnp.zeros((32, LANES), F32)
    z1_ref[6] = jnp.concatenate([low, high, rest], 0).astype(BF16)


def prepare(rows, link_rows):
    return pl.pallas_call(
        prepare_kernel,
        out_shape=(
            shape((24, NV, LANES), BF16),
            shape((26, NV, LANES), BF16),
            shape((6, NV, LANES), BF16),
            shape((7, NV, LANES), BF16),
        ),
        in_specs=[VMEM] * 2,
        out_specs=(VMEM,) * 4,
        scratch_shapes=[
            pltpu.VMEM((NV * NK, LANES), F32),
            pltpu.VMEM((576, LANES), F32),
        ],
        compiler_params=params(6),
        cost_estimate=pl.CostEstimate(flops=2000000000, bytes_accessed=3000000, transcendentals=0),
        name="prepare",
    )(rows, link_rows)


def line_coefficients(rows, first):
    half = rows * 0.5
    swapped = pltpu.roll(half, HALF, 1)
    return jnp.where(first, half, swapped), jnp.where(first, swapped, half)


def lane_masks():
    lane = lax.broadcasted_iota(jnp.int32, (1, LANES), 1)
    return lane, lane < HALF, jnp.where(lane < HALF, -1.0, 1.0).astype(F32)


def derivative(mu, neighbour, tables, zy, store):
    upr, upi, dnr, dni = tables
    out = [None] * 3
    for c in range(COL):
        here, swap = neighbour(c, 1)
        for r in range(3):
            at = mu * 9 + r * 3 + c
            term = here * upr[zy, at:at + 1, :] + swap * upi[zy, at:at + 1, :]
            out[r] = term if out[r] is None else out[r] + term
    for c in range(COL):
        here, swap = neighbour(c, -1)
        for r in range(3):
            at = mu * 9 + c * 3 + r
            term = here * dnr[zy, at:at + 1, :] - swap * dni[zy, at:at + 1, :]
            out[r] = out[r] - term
    for r in range(3):
        store(r, out[r].astype(BF16))


def local_kernel(
    momentum_ref, v_ref, l_ref, w_ref, ext, exts, upr, upi, dnr, dni,
    wide, lwide, real, imag, cos_ref, sin_ref,
):
    lane, first, sign = lane_masks()
    at = lax.broadcasted_iota(jnp.int32, (NZY, LANES), 0)
    x = lax.broadcasted_iota(jnp.int32, (NZY, LANES), 1) & (HALF - 1)
    y = lax.axis_index("gy").astype(jnp.int32) * HY + (at & (HY - 1))
    z = lax.axis_index("gz").astype(jnp.int32) * DZ + (at >> 1)
    frac_x = ((momentum_ref[0] * x) & (EXT_X - 1)).astype(F32) / EXT_X
    frac_y = ((momentum_ref[1] * y) & (EXT_Y - 1)).astype(F32) / EXT_Y
    frac_z = ((momentum_ref[2] * z) & (EXT_Z - 1)).astype(F32) / EXT_Z
    angle = 2.0 * math.pi * (frac_z + frac_y + frac_x)
    cos_ref[0:NZY, :] = jnp.cos(angle)
    sin_ref[0:NZY, :] = -sign * jnp.sin(angle)

    wide[...] = v_ref[...].astype(F32)
    for c in range(COL):
        for z in range(DZ):
            for y in range(HY):
                tile = wide[pl.ds((c * DZ + z) * HY + y, NV, stride=NK), :]
                ext[c, z + 1, y + 1] = tile
                exts[c, z + 1, y + 1] = pltpu.roll(tile, HALF, 1)

    lwide[0:432, :] = l_ref[...].astype(F32)
    lwide[432:LINES, :] = jnp.zeros((LINES - 432, LANES), F32)
    re, im = line_coefficients(lwide[...], first)
    real[...] = re
    imag[...] = im
    for zy in range(NZY):
        z, y = zy // HY, zy % HY
        pick = pl.ds(zy, 27, stride=NZY)
        upr[zy, 0:27, :] = real[pick, :]
        upi[zy, 0:27, :] = imag[pick, :] * sign
        pick = pl.ds(zy, 9, stride=NZY)
        dnr[zy, 0:9, :] = pltpu.roll(real[pick, :], 1, 1)
        dni[zy, 0:9, :] = pltpu.roll(imag[pick, :], 1, 1) * sign
        if y:
            pick = pl.ds(9 * NZY + zy - 1, 9, stride=NZY)
            dnr[zy, 9:18, :] = real[pick, :]
            dni[zy, 9:18, :] = imag[pick, :] * sign
        if z:
            pick = pl.ds(18 * NZY + zy - HY, 9, stride=NZY)
            dnr[zy, 18:27, :] = real[pick, :]
            dni[zy, 18:27, :] = imag[pick, :] * sign

    wrap_up = (lane == HALF - 1) | (lane == LANES - 1)
    wrap_down = (lane == 0) | (lane == HALF)

    def site(zy, carry):
        z = lax.div(zy, HY) + 1
        y = lax.rem(zy, HY) + 1

        def neighbour(c, step):
            here, swap = ext[c, z, y], exts[c, z, y]
            a = pltpu.roll(here, (-step) % LANES, 1)
            b = pltpu.roll(swap, (-step) % LANES, 1)
            wrap = wrap_up if step == 1 else wrap_down
            return jnp.where(wrap, b, a), jnp.where(wrap, a, b)

        def store(r, value):
            column = pl.multiple_of((r * NZY + zy) * LANES, LANES)
            w_ref[0, :, pl.ds(column, LANES)] = value

        derivative(0, neighbour, (upr, upi, dnr, dni), zy, store)
        cosine = cos_ref[pl.ds(zy, 1), :]
        sine = sin_ref[pl.ds(zy, 1), :]
        for c in range(COL):
            column = pl.multiple_of((c * NZY + zy) * LANES, LANES)
            phased = ext[c, z, y] * cosine + exts[c, z, y] * sine
            w_ref[1, :, pl.ds(column, LANES)] = phased.astype(BF16)
        return carry

    lax.fori_loop(0, NZY, site, 0)


EXTENDED = (COL, DZ + 2, HY + 2, NV, LANES)
TABLE = (NZY, 40, LANES)
LINES = 576


def local_terms(momentum, rows, link_rows):
    line = pltpu.VMEM((LINES, LANES), F32)
    return pl.pallas_call(
        local_kernel,
        out_shape=(shape((4, NV, KDIM), BF16),)
        + (shape(EXTENDED, F32),) * 2
        + (shape(TABLE, F32),) * 4,
        in_specs=[SMEM] + [VMEM] * 2,
        out_specs=(VMEM,) * 7,
        scratch_shapes=[
            pltpu.VMEM((NV * NK, LANES), F32),
            line,
            line,
            line,
            pltpu.VMEM((NZY + 8, LANES), F32),
            pltpu.VMEM((NZY + 8, LANES), F32),
        ],
        compiler_params=params(8),
        cost_estimate=pl.CostEstimate(flops=6000000000, bytes_accessed=6000000, transcendentals=0),
        name="local_terms",
    )(momentum, rows, link_rows)


def border_kernel(
    mu, before_ref, e_ref, s_ref, upr, upi, r_ref, i_ref, ahead_ref, behind_ref,
    w_ref, ext, exts, dnr, dni, lwide, real, imag,
):
    lane, first, sign = lane_masks()

    def put(c, z, y, tile):
        tile = tile.astype(F32)
        ext[c, z, y] = tile
        exts[c, z, y] = pltpu.roll(tile, HALF, 1)

    for c in range(COL):
        if mu == 1:
            for z in range(DZ):
                put(c, z + 1, HY + 1, ahead_ref[c * DZ + z])
                put(c, z + 1, 0, behind_ref[c * DZ + z])
        else:
            for y in range(HY):
                put(c, DZ + 1, y + 1, ahead_ref[c * HY + y])
                put(c, 0, y + 1, behind_ref[c * HY + y])

    if mu == 1:
        lwide[...] = jnp.concatenate([behind_ref[24], behind_ref[25]], 0).astype(F32)
    else:
        lwide[0:64, :] = behind_ref[6].astype(F32)
        lwide[64:128, :] = jnp.zeros((64, LANES), F32)
    re, im = line_coefficients(lwide[...], first)
    real[...] = re
    imag[...] = im * sign
    if mu == 1:
        for z in range(DZ):
            pick = pl.ds(z, 9, stride=DZ)
            dnr[z * HY, 9:18, :] = real[pick, :]
            dni[z * HY, 9:18, :] = imag[pick, :]
    else:
        for y in range(HY):
            pick = pl.ds(16 * y, 9)
            dnr[y, 18:27, :] = real[pick, :]
            dni[y, 18:27, :] = imag[pick, :]

    def site(zy, carry):
        z = lax.div(zy, HY) + 1
        y = lax.rem(zy, HY) + 1

        def neighbour(c, step):
            at = (c, z, y + step) if mu == 1 else (c, z + step, y)
            return ext[at], exts[at]

        def store(r, value):
            column = pl.multiple_of((r * NZY + zy) * LANES, LANES)
            w_ref[mu + 1, :, pl.ds(column, LANES)] = value

        derivative(mu, neighbour, (upr, upi, dnr, dni), zy, store)
        return carry

    lax.fori_loop(0, NZY, site, 0)


def border_terms(mu, w, ext, exts, upr, upi, dnr, dni, ahead, behind):
    line = pltpu.VMEM((128, LANES), F32)
    w, ext, exts, dnr, dni = pl.pallas_call(
        functools.partial(border_kernel, mu),
        out_shape=(shape((4, NV, KDIM), BF16),)
        + (shape(EXTENDED, F32),) * 2
        + (shape(TABLE, F32),) * 2,
        in_specs=[VMEM] * 9,
        out_specs=(VMEM,) * 5,
        input_output_aliases={0: 0, 1: 1, 2: 2, 5: 3, 6: 4},
        scratch_shapes=[line, line, line],
        compiler_params=params(4),
        cost_estimate=pl.CostEstimate(flops=3000000000, bytes_accessed=3000000, transcendentals=0),
        name="border_y" if mu == 1 else "border_z",
    )(w, ext, exts, upr, upi, dnr, dni, ahead, behind)
    return w, ext, exts, upr, upi, dnr, dni


def fill_right(counts, blocks, wide, right):
    total = sum(counts)
    lane, first, sign = lane_masks()
    start = 0
    for block, count in zip(blocks, counts):
        wide[0:count * NK, :] = block[...].astype(F32)
        for k in range(NK):
            tile = wide[pl.ds(k, count, stride=NK), :]
            swap = pltpu.roll(tile, HALF, 1) * sign
            right[start:start + count, k * LANES:(k + 1) * LANES] = tile.astype(BF16)
            right[total + start:total + start + count, k * LANES:(k + 1) * LANES] = swap.astype(BF16)
        start += count


def dot_halves(w_ref, right, keep_ref, send_ref, product):
    left = w_ref[...].reshape(4 * NV, KDIM)
    dots = lax.dot_general(left, right[...], (((1,), (1,)), ((), ())), preferred_element_type=F32)
    product[...] = dots.reshape(2, 2 * NV, dots.shape[1])
    mine = lax.axis_index("gz").astype(jnp.int32) & 1
    keep_ref[...] = product[mine]
    send_ref[...] = product[1 - mine]


def right_kernel(counts, *refs):
    n = len(counts)
    fill_right(counts, refs[:n], refs[n + 1], refs[n])


def right_side(blocks):
    counts = tuple(b.shape[0] // NK for b in blocks)
    return pl.pallas_call(
        functools.partial(right_kernel, counts),
        out_shape=shape((2 * sum(counts), KDIM), BF16),
        in_specs=[VMEM] * len(blocks),
        out_specs=VMEM,
        scratch_shapes=[pltpu.VMEM((max(counts) * NK, LANES), F32)],
        compiler_params=params(4),
        cost_estimate=pl.CostEstimate(flops=2000000000, bytes_accessed=4000000, transcendentals=0),
        name="right_side",
    )(*blocks)


def near_kernel(w_ref, right_ref, keep_ref, send_ref, product):
    dot_halves(w_ref, right_ref, keep_ref, send_ref, product)


def far_kernel(counts, w_ref, *refs):
    n = len(counts)
    keep_ref, send_ref, wide, right, product = refs[n:]
    fill_right(counts, refs[:n], wide, right)
    dot_halves(w_ref, right, keep_ref, send_ref, product)


def contract_near(w, right):
    columns = right.shape[0]
    out = shape((2 * NV, columns), F32)
    return pl.pallas_call(
        near_kernel,
        out_shape=(out, out),
        in_specs=[VMEM] * 2,
        out_specs=(VMEM, VMEM),
        scratch_shapes=[pltpu.VMEM((2, 2 * NV, columns), F32)],
        compiler_params=params(4),
        cost_estimate=pl.CostEstimate(
            flops=2 * 256 * columns * KDIM, bytes_accessed=4000000, transcendentals=0
        ),
        name="contract_near",
    )(w, right)


def contract_far(w, blocks):
    counts = tuple(b.shape[0] // NK for b in blocks)
    columns = 2 * sum(counts)
    out = shape((2 * NV, columns), F32)
    return pl.pallas_call(
        functools.partial(far_kernel, counts),
        out_shape=(out, out),
        in_specs=[VMEM] * (1 + len(blocks)),
        out_specs=(VMEM, VMEM),
        scratch_shapes=[
            pltpu.VMEM((max(counts) * NK, LANES), F32),
            pltpu.VMEM((columns, KDIM), BF16),
            pltpu.VMEM((2, 2 * NV, columns), F32),
        ],
        compiler_params=params(5),
        cost_estimate=pl.CostEstimate(
            flops=2 * 256 * columns * KDIM, bytes_accessed=4000000, transcendentals=0
        ),
        name="contract_far",
    )(w, *blocks)


def finish_kernel(scale, other, dirs_ref, rows_ref, *refs):
    out_ref, lines, sem = refs[-3:]
    shift = lax.axis_index("vec").astype(jnp.int32) * HALF
    half = (lax.axis_index("gz").astype(jnp.int32) & 1) ^ other
    slots = [
        sum(jnp.where(dirs_ref[o] == mu, o, 0) for o in range(3)).astype(jnp.int32)
        for mu in range(3)
    ]
    places = [jnp.where(half == 0, slots[0], slots[1]), jnp.where(half == 0, 3, slots[2])]
    rows = rows_ref[...]
    copies = []
    for part in range(2):
        near = rows[:, part * 192:(part + 1) * 192]
        far = rows[:, 384 + part * 64:384 + (part + 1) * 64]
        line = jnp.concatenate([near[:, 0:128], far, near[:, 128:192]], 1) * scale
        line = pltpu.roll(line, shift, 1)
        for which in range(2):
            lines[which, part] = line[which * NV:(which + 1) * NV]
            copy = pltpu.make_async_copy(
                lines.at[which, part], out_ref.at[places[which], part], sem.at[which, part]
            )
            copy.start()
            copies.append(copy)
    for copy in copies:
        copy.wait()


def finish(directions, rows, scale, so_far=None):
    other = so_far is not None
    return pl.pallas_call(
        functools.partial(finish_kernel, scale, int(other)),
        out_shape=shape((4, 2, NV, 256), F32),
        in_specs=[SMEM, VMEM] + [HBM] * other,
        out_specs=HBM,
        input_output_aliases={2: 0} if other else {},
        scratch_shapes=[pltpu.VMEM((2, 2, NV, 256), F32), pltpu.SemaphoreType.DMA((2, 2))],
        compiler_params=params(4),
        cost_estimate=pl.CostEstimate(flops=200000, bytes_accessed=1000000, transcendentals=0),
        name="finish_other" if other else "finish_mine",
    )(directions, rows, *([so_far] if other else []))


def permuted(value, axis, target):
    size = lax.axis_size(axis)
    return lax.ppermute(value, axis, [(source, target(source)) for source in range(size)])


def crossed(value, flip, turn):
    pairs = []
    for gz in range(4):
        for gy in range(8):
            x, z = gy % 4, (gy // 4) * 2 + gz // 2
            if gz % 2 == turn:
                x ^= flip
            else:
                z ^= flip
            pairs.append((gz * 8 + gy, ((z % 2) * 2 + gz % 2) * 8 + (z // 2) * 4 + x))
    return lax.ppermute(value, ("gz", "gy"), pairs)


def four_sum(own, opposite, side, other):
    pair = side.astype(F32) + other.astype(F32)
    return pair + (own.astype(F32) + opposite.astype(F32))


def body(vectors, links, momentum, directions):
    rows = vectors.reshape(NV * NK, LANES)
    link_rows = links.reshape(27 * NZY, LANES)
    mid = NV * NK // 2
    prev = permuted(rows, "vec", lambda s: (s + 1) % 4)
    next_ = permuted(rows, "vec", lambda s: (s - 1) % 4)

    y0, y1, z0, z1 = prepare(rows, link_rows)
    yp = permuted(y0, "gy", lambda s: (s - 1) % 8)
    ym = permuted(y1, "gy", lambda s: (s + 1) % 8)
    zp = permuted(z0, "gz", lambda s: (s - 1) % 4)
    z1, zp = lax.optimization_barrier((z1, zp))
    zm = permuted(z1, "gz", lambda s: (s + 1) % 4)
    partial = local_terms(momentum, rows, link_rows)

    far_low = permuted(prev[:mid], "vec", lambda s: (s + 1) % 4)
    far_high = permuted(next_[mid:], "vec", lambda s: (s - 1) % 4)

    right = right_side([rows, next_, prev])
    zm, right = lax.optimization_barrier((zm, right))
    partial = border_terms(2, *partial, zp, zm)
    w = border_terms(1, *partial, yp, ym)[0]

    mate = lambda v: permuted(v, "gz", lambda s: s ^ 1)

    def chip_sum(keep, send):
        return (keep + mate(send)).astype(BF16)

    near = chip_sum(*contract_near(w, right))
    far = chip_sum(*contract_far(w, [far_low, far_high]))
    chip = jnp.concatenate([near, far], 1)
    row = four_sum(chip, *[crossed(chip, flip, 1) for flip in (2, 1, 3)]).astype(BF16)
    plane = four_sum(row, *[crossed(row, flip, 0) for flip in (2, 1, 3)])
    scale = 1.0 / math.sqrt(EXT_X * EXT_Y * EXT_Z)
    mine = finish(directions, plane, scale)
    return finish(directions, mate(plane), scale, mine)


def solution(mesh):
    in_specs = (P("vec", None, "gz", "gy", None), P(None, None, None, "gz", "gy", None), P(), P())
    out_specs = P(None, None, "vec", None)
    return jax.shard_map(body, mesh=mesh, in_specs=in_specs, out_specs=out_specs, check_vma=False)
```
